32 devices in a mesh: replica: 2 (over y), width: 2 (over core), hidden: 8 (over z, x).
Axes of the slice: x: 2, y: 2, z: 4, core: 2. Of those that a mesh axis runs over, the one named last changes fastest.
Arguments:
- acts: bfloat16 [160, 8192], P(('replica', 'hidden'), 'width'), parts along dimension 0, may hold values from -6 to 6
- gate_codes: bfloat16 [8192, 26624], P('width', 'hidden'), may hold values from -4 to 4
- gate_scales: float32 [256, 26624], P('width', 'hidden'), may hold values from 0.0055242716 to 0.022097087
- up_codes: bfloat16 [8192, 26624], P('width', 'hidden'), may hold values from -4 to 4
- up_scales: float32 [256, 26624], P('width', 'hidden'), may hold values from 0.0055242716 to 0.022097087
- down_codes: bfloat16 [26624, 8192], P('hidden', 'width'), may hold values from -4 to 4
- down_scales: float32 [832, 8192], P('hidden', 'width'), may hold values from 0.006128629 to 0.024514517
Outputs:
- mixed: bfloat16 [160, 8192], P(('replica', 'hidden'), 'width'), parts along dimension 0
The draws below stay inside these ranges and needn't reach their ends.
There are 2 independent parts, one for each index of `replica`. The reference program is written for one: setup_inputs(seed, part) draws one part's arguments, and reference() takes and returns one part's arrays. A program takes and returns all parts, laid end to end along the dimension named above; an argument that names none is the same for every part. Nothing has to cross between parts.
All inputs are finite; a program needn't handle non-finite values.
Results may differ from the reference program's by a relative error of at most 0.0072.
Values may be sent and summed in bfloat16 or wider, within the bound.
No kernel may reach another device: no remote copies, remote signals or barrier semaphores. Data moves between devices by JAX's collectives and lax.ppermute only.
A program may use at most 320 MiB of HBM per device.

```python
import math
import jax
import jax.numpy as jnp

D = 8192
FF = 26624
BLOCK = 32
ROWS = 80


def block_scale(stream_key, extent, split, least, high):
    def one(position, blocks):
        steps = jax.random.uniform(jax.random.fold_in(jax.random.fold_in(stream_key, 6), position), (blocks,), jnp.float32, least / len(split), high / len(split))
        return jnp.repeat(jnp.exp(steps), extent[position] // blocks).reshape((-1,) + (1,) * (len(extent) - position - 1))

    loudness = one(*split[0])
    for cut in split[1:]:
        loudness = loudness * one(*cut)
    return loudness


def normal_values(stream_key, dims, deviation, limit, shards=(), kind=jnp.bfloat16):
    entries = deviation * jax.random.normal(stream_key, dims, jnp.float32)
    if shards:
        entries = entries * block_scale(stream_key, dims, shards, -0.22, 0.18)
    return jnp.clip(entries, -limit, limit).astype(kind)


def setup_inputs(seed: int = 0, part: int = 0) -> dict:
    splits = jax.random.split(jax.random.key(seed), 8)
    own_keys = jax.random.split(jax.random.fold_in(splits[7], part), 8)
    return {
        "acts": normal_values(own_keys[0], (ROWS, D), 1.0, 6.0, ((0, 8), (1, 2))),
        "gate_codes": normal_values(splits[1], (D, FF), 1.0, 4.0, ((0, 2), (1, 8))),
        "gate_scales": jnp.clip(jnp.exp(math.log(0.022097087) - 1.3862944 * jax.random.uniform(splits[2], (D // BLOCK, FF), jnp.float32) ** block_scale(splits[2], (D // BLOCK, FF), ((0, 2), (1, 8)), -0.2, 0.2)), 0.0055242716, 0.022097087),
        "up_codes": normal_values(splits[3], (D, FF), 1.0, 4.0, ((0, 2), (1, 8))),
        "up_scales": jnp.clip(jnp.exp(math.log(0.022097087) - 1.3862944 * jax.random.uniform(splits[4], (D // BLOCK, FF), jnp.float32) ** block_scale(splits[4], (D // BLOCK, FF), ((0, 2), (1, 8)), -0.2, 0.2)), 0.0055242716, 0.022097087),
        "down_codes": normal_values(splits[5], (FF, D), 1.0, 4.0, ((0, 8), (1, 2))),
        "down_scales": jnp.clip(jnp.exp(math.log(0.024514517) - 1.3862944 * jax.random.uniform(splits[6], (FF // BLOCK, D), jnp.float32) ** block_scale(splits[6], (FF // BLOCK, D), ((0, 8), (1, 2)), -0.2, 0.2)), 0.006128629, 0.024514517),
    }


def dequant(codes, scales):
    groups = scales.shape[0]
    shaped = codes.reshape(groups, codes.shape[0] // groups, codes.shape[1]).astype(jnp.float32)
    return (shaped * scales[:, None, :]).reshape(codes.shape).astype(jnp.bfloat16)


def reference(acts, gate_codes, gate_scales, up_codes, up_scales, down_codes, down_scales):
    gate = jnp.dot(acts, dequant(gate_codes, gate_scales), preferred_element_type=jnp.float32)
    up = jnp.dot(acts, dequant(up_codes, up_scales), preferred_element_type=jnp.float32)
    hidden = (jax.nn.silu(gate) * up).astype(jnp.bfloat16)
    mixed = jnp.dot(hidden, dequant(down_codes, down_scales), preferred_element_type=jnp.float32)
    return mixed.astype(jnp.bfloat16)
```

```python
import functools

import jax
import jax.numpy as jnp
from jax import lax
from jax.experimental import pallas as pl
from jax.experimental.pallas import tpu as pltpu
from jax.sharding import PartitionSpec as P

BF16, F32 = jnp.bfloat16, jnp.float32
MIB = 1 << 20
TILE = 8


def divisor(extent, limit, step):
    for size in range(limit - limit % step, 0, -step):
        if extent % size == 0:
            return size
    return extent


def whole(count):
    return [pl.BlockSpec(memory_space=pltpu.VMEM)] * count


def call(body, out_shape, operands, name, limit, scratch=(), flops=0):
    single = not isinstance(out_shape, (list, tuple))
    shapes = [out_shape] if single else out_shape
    moved = sum(x.size * x.dtype.itemsize for x in operands)
    return pl.pallas_call(
        body,
        in_specs=whole(len(operands)),
        out_specs=whole(1)[0] if single else whole(len(shapes)),
        out_shape=out_shape,
        scratch_shapes=list(scratch),
        compiler_params=pltpu.CompilerParams(vmem_limit_bytes=limit),
        cost_estimate=pl.CostEstimate(flops=flops, bytes_accessed=moved, transcendentals=0),
        name=name,
    )(*operands)


def pack_body(a_ref, o_ref):
    m, width = a_ref.shape
    rest = m - TILE
    piece = rest * width // TILE
    a = a_ref[...].astype(F32)
    o_ref[:, :width] = a[:TILE].astype(BF16)
    left = [a[TILE:, k * piece : (k + 1) * piece] for k in range(TILE // rest)]
    o_ref[:, width:] = jnp.concatenate(left, axis=0).astype(BF16)


def unpack_rows(block, rest, store):
    width = block.shape[1] * TILE // (TILE + rest)
    piece = rest * width // TILE
    store(0, 0, block[:, :width])
    for k in range(TILE // rest):
        store(TILE, k * piece, block[k * rest : (k + 1) * rest, width:])


def pack_all(total, first, rest, blocks):
    width = total.shape[1]
    piece = rest * width // TILE
    base = blocks * TILE + first * rest
    left = [total[base : base + rest, k * piece : (k + 1) * piece] for k in range(TILE // rest)]
    return total[first * TILE : (first + 1) * TILE, :], jnp.concatenate(left, axis=0)


def dequant(codes, scales):
    depth, width = codes.shape
    groups = scales.shape[0]
    shaped = codes.astype(F32).reshape(groups, depth // groups, width)
    return (shaped * scales[:, None, :]).astype(BF16).reshape(depth, width)


def project(a_ref, codes_ref, scales_ref, store):
    depth, width = codes_ref.shape
    block = depth // scales_ref.shape[0]
    columns = divisor(width, 1664, 128)
    rows = divisor(depth, 512, 8 * block)

    def step(j):
        cols = pl.ds(j * columns if isinstance(j, int) else pl.multiple_of(j * columns, columns), columns)
        total = jnp.zeros((a_ref.shape[0], columns), F32)
        for k in range(0, depth, rows):
            w = dequant(codes_ref[k : k + rows, cols], scales_ref[k // block : (k + rows) // block, cols])
            total += jnp.dot(a_ref[:, k : k + rows], w, preferred_element_type=F32)
        store(cols, total)

    if width == columns:
        step(0)
    else:
        pl.loop(0, width // columns)(step)


def gate_body(count, rest, *refs):
    blocks, (codes, scales), (acts, own, sent), wide = refs[:count], refs[count : count + 2], refs[count + 2 : count + 5], refs[count + 5]
    total = sum(b.shape[0] for b in blocks) // TILE
    at = 0
    for ref in blocks:
        for i in range(ref.shape[0] // TILE):
            def store(row, column, values):
                first = at * TILE if row == 0 else total * TILE + at * rest
                wide[first : first + values.shape[0], column : column + values.shape[1]] = values
            unpack_rows(ref[i * TILE : (i + 1) * TILE, :].astype(F32), rest, store)
            at += 1
    acts[...] = wide[...].astype(BF16)
    up_body(acts, codes, scales, own, sent)


def up_body(acts, codes, scales, own, sent):
    def store(cols, total):
        own[:, cols] = total
        sent[:, cols] = total.astype(BF16)

    project(acts, codes, scales, store)


def down_body(rest, blocks, kept, *refs):
    gate, gate_other, up, up_other, codes, scales = refs[:6]
    outs, (hidden, terms) = refs[6:-2], refs[-2:]
    width = divisor(hidden.shape[1], 512, 128)
    for c in range(0, hidden.shape[1], width):
        cols = slice(c, c + width)
        g = gate[:, cols] + gate_other[:, cols].astype(F32)
        u = up[:, cols] + up_other[:, cols].astype(F32)
        hidden[:, cols] = (jax.nn.silu(g) * u).astype(BF16)

    def store(cols, total):
        terms[:, cols] = total

    project(hidden, codes, scales, store)
    width = terms.shape[1]
    for i in range(blocks):
        main, left = pack_all(terms, i, rest, blocks)
        out, at = (outs[0], i) if i < kept else (outs[1], i - kept)
        out[at * TILE : (at + 1) * TILE, :width] = main.astype(out.dtype)
        out[at * TILE : (at + 1) * TILE, width:] = left.astype(out.dtype)


def add_body(mine, other, first, *later):
    first[...] = mine[:TILE, :] + other[:TILE, :].astype(F32)
    for i, ref in enumerate(later):
        rows = slice((i + 1) * TILE, (i + 2) * TILE)
        ref[...] = (mine[rows, :] + other[rows, :].astype(F32)).astype(BF16)


def last_body(*refs):
    out = refs[-1]
    total = refs[0][...]
    for ref in refs[1:-1]:
        total += ref[...].astype(F32)

    def store(row, column, values):
        out[row : row + values.shape[0], column : column + values.shape[1]] = values.astype(out.dtype)

    unpack_rows(total, out.shape[0] - TILE, store)


def local(peers, acts, gate_codes, gate_scales, up_codes, up_scales, down_codes, down_scales):
    m, width = acts.shape
    units = gate_codes.shape[1]
    rest = m - TILE
    dense = width + rest * width // TILE
    rows = peers * m
    sds = jax.ShapeDtypeStruct
    pair = peers == 8
    far = peers // 2

    def flip(x):
        return lax.ppermute(x, "hidden", [(h, h ^ 1) for h in range(peers)])

    def along(x, s):
        return lax.ppermute(x, "hidden", [(h, (h + 2 * s) % peers) for h in range(peers)])

    def swap(x):
        return lax.ppermute(x, "width", [(0, 1), (1, 0)])

    def in_vmem(x):
        return pltpu.with_memory_space_constraint(x, pltpu.VMEM)

    packed = call(pack_body, sds((TILE, dense), BF16), [acts], "pack", 4 * MIB)
    if pair:
        line = [packed] + [along(packed, s) for s in range(1, far)]
        blocks = line + [flip(x) for x in line]
    else:
        blocks = [lax.all_gather(packed, "hidden", axis=0, tiled=True)]
    work = 2 * rows * width * units
    spare = 4 * rows * (width + 3 * units) + 12 * MIB
    acts_all, gate, gate_sent = call(
        functools.partial(gate_body, len(blocks), rest),
        [sds((rows, width), BF16), sds((rows, units), F32), sds((rows, units), BF16)],
        blocks + [in_vmem(gate_codes), gate_scales],
        "gate",
        min(spare, 40 * MIB),
        scratch=[pltpu.VMEM((rows, width), F32)],
        flops=work,
    )
    gate_other = swap(gate_sent)
    up, up_sent = call(
        up_body,
        [sds((rows, units), F32), sds((rows, units), BF16)],
        [acts_all, in_vmem(up_codes), up_scales],
        "up",
        min(spare, 40 * MIB),
        flops=work,
    )
    up_other = swap(up_sent)
    kept = far if pair else peers
    outs = [sds((kept * TILE, dense), F32)] + ([sds((far * TILE, dense), BF16)] if pair else [])
    parts = call(
        functools.partial(down_body, rest, peers, kept),
        outs,
        [gate, gate_other, up, up_other, in_vmem(down_codes), down_scales],
        "down",
        min(4 * rows * (3 * width + 3 * units) + 8 * MIB, 48 * MIB),
        scratch=[pltpu.VMEM((rows, units), BF16), pltpu.VMEM((rows, width), F32)],
        flops=work,
    )
    if pair:
        mine, sent = parts
        other = flip(sent)
        sums = call(
            add_body,
            [sds((TILE, dense), F32)] + [sds((TILE, dense), BF16)] * (far - 1),
            [mine, other],
            "add",
            8 * MIB,
        )
        terms = [sums[0]] + [along(x, far - s) for s, x in zip(range(1, far), sums[1:])]
    else:
        terms = [lax.psum_scatter(parts[0], "hidden", scatter_dimension=0, tiled=True)]
    return call(last_body, sds((m, width), BF16), terms, "last", 8 * MIB)


def solution(mesh):
    placed = (
        P(("replica", "hidden"), "width"),
        P("width", "hidden"),
        P("width", "hidden"),
        P("width", "hidden"),
        P("width", "hidden"),
        P("hidden", "width"),
        P("hidden", "width"),
    )
    return jax.shard_map(
        functools.partial(local, mesh.shape["hidden"]),
        mesh=mesh,
        in_specs=placed,
        out_specs=P(("replica", "hidden"), "width"),
        check_vma=False,
    )
```

```python
import functools
import math

import jax
import jax.numpy as jnp
from jax import lax
from jax.experimental import pallas as pl
from jax.experimental.pallas import tpu as pltpu
from jax.sharding import PartitionSpec as P

BF16, F32 = jnp.bfloat16, jnp.float32
MIB = 1 << 20
PACK_WEIGHT, GATE_WEIGHT, UP_WEIGHT = 60_000_000_000, 10_000_000_000, 10_000_000_000
TILE = 8


def divisor(extent, limit, step):
    for size in range(limit - limit % step, 0, -step):
        if extent % size == 0:
            return size
    return extent


def whole(count):
    return [pl.BlockSpec(memory_space=pltpu.VMEM)] * count


def call(body, out_shape, operands, name, scratch=(), flops=0, apart=(), spare=2 * MIB):
    single = not isinstance(out_shape, (list, tuple))
    shapes = [out_shape] if single else out_shape
    held = [x for x in scratch if getattr(x, "dtype", None) in (BF16, F32)]
    limit = spare + sum(math.prod(x.shape) * jnp.dtype(x.dtype).itemsize for x in held)
    moved = sum(x.size * x.dtype.itemsize for x in operands)
    return pl.pallas_call(
        body,
        in_specs=[pl.BlockSpec(memory_space=pl.ANY if i in apart else pltpu.VMEM) for i in range(len(operands))],
        out_specs=whole(1)[0] if single else whole(len(shapes)),
        out_shape=out_shape,
        scratch_shapes=list(scratch),
        compiler_params=pltpu.CompilerParams(vmem_limit_bytes=limit),
        cost_estimate=pl.CostEstimate(flops=flops, bytes_accessed=moved, transcendentals=0),
        name=name,
    )(*operands)


def pack_body(a_ref, o_ref):
    m, width = a_ref.shape
    rest = m - TILE
    piece = rest * width // TILE
    a = a_ref[...].astype(F32)
    o_ref[:, :width] = a[:TILE].astype(BF16)
    left = [a[TILE:, k * piece : (k + 1) * piece] for k in range(TILE // rest)]
    o_ref[:, width:] = jnp.concatenate(left, axis=0).astype(BF16)


def unpack_rows(block, rest, store):
    width = block.shape[1] * TILE // (TILE + rest)
    piece = rest * width // TILE
    store(0, 0, block[:, :width])
    for k in range(TILE // rest):
        store(TILE, k * piece, block[k * rest : (k + 1) * rest, width:])


def pack_all(total, first, rest, blocks):
    width = total.shape[1]
    piece = rest * width // TILE
    base = blocks * TILE + first * rest
    left = [total[base : base + rest, k * piece : (k + 1) * piece] for k in range(TILE // rest)]
    return total[first * TILE : (first + 1) * TILE, :], jnp.concatenate(left, axis=0)


def dequant(codes, scales):
    depth, width = codes.shape
    groups = scales.shape[0]
    shaped = codes.astype(F32).reshape(groups, depth // groups, width)
    return (shaped * scales[:, None, :]).astype(BF16).reshape(depth, width)


def pieces(width, count):
    if width % 128 or width < 128 * 2 * count:
        return [(0, width)]
    tiles = width // 128
    ends = [0, tiles // 2, (3 * tiles + 2) // 4, tiles] if count == 3 else [tiles * k // count for k in range(count + 1)]
    return [(128 * a, 128 * (b - a)) for a, b in zip(ends, ends[1:])]


def project(a_ref, codes_ref, at, scales_ref, start, size):
    depth = codes_ref.shape[0]
    block = depth // scales_ref.shape[0]
    rows = divisor(depth, 512, 8 * block)
    total = jnp.zeros((a_ref.shape[0], size), F32)
    for k in range(0, depth, rows):
        w = dequant(codes_ref[k : k + rows, at : at + size], scales_ref[k // block : (k + rows) // block, start : start + size])
        total += jnp.dot(a_ref[:, k : k + rows], w, preferred_element_type=F32)
    return total


def fetch(source, start, size, target, at, done):
    copy = pltpu.make_async_copy(source.at[:, start : start + size], target.at[:, at : at + size], done)
    copy.start()
    return copy


def fetch_rest(source, cuts, target, done):
    ahead = cuts[0][1]
    return [fetch(source, start, size, target, start - ahead, done.at[i]) for i, (start, size) in enumerate(cuts[1:])]


def gate_body(count, rest, *refs):
    blocks = refs[:count]
    codes, scales, later, acts, own, sent, head, wide, done = refs[count:]
    copy = fetch(later, 0, head.shape[1], head, 0, done)
    total = sum(b.shape[0] for b in blocks) // TILE
    at = 0
    for ref in blocks:
        for i in range(ref.shape[0] // TILE):
            def store(row, column, values):
                first = at * TILE if row == 0 else total * TILE + at * rest
                wide[first : first + values.shape[0], column : column + values.shape[1]] = values
            unpack_rows(ref[i * TILE : (i + 1) * TILE, :].astype(F32), rest, store)
            at += 1
    acts[...] = wide[...].astype(BF16)
    for start, size in pieces(codes.shape[1], 2):
        total = project(acts, codes, start, scales, start, size)
        own[:, start : start + size] = total
        sent[:, start : start + size] = total.astype(BF16)
    copy.wait()


def up_body(cuts, acts, first, codes, scales, later, own, sent, head, *refs):
    ahead = first.shape[1]
    rest = fetch_rest(codes, cuts, *refs[1:]) if len(cuts) > 1 else []
    copy = fetch(later, 0, head.shape[1], head, 0, refs[0])
    for i, (start, size) in enumerate(cuts):
        if i:
            rest[i - 1].wait()
        total = project(acts, refs[1] if i else first, start - ahead if i else 0, scales, start, size)
        own[:, start : start + size] = total
        sent[:, start : start + size] = total.astype(BF16)
    copy.wait()


def down_body(cuts, rest, blocks, kept, two, gate, gate_other, up, up_other, head, codes, scales, *refs):
    outs, (hidden, terms) = refs[: 1 + two], refs[1 + two : 3 + two]
    held = refs[3 + two :]
    ahead = head.shape[1]
    copies = fetch_rest(codes, cuts, *held) if held else []
    width = divisor(hidden.shape[1], 512, 128)
    for c in range(0, hidden.shape[1], width):
        cols = slice(c, c + width)
        g = gate[:, cols] + gate_other[:, cols].astype(F32)
        u = up[:, cols] + up_other[:, cols].astype(F32)
        hidden[:, cols] = (jax.nn.silu(g) * u).astype(BF16)
    for i, (start, size) in enumerate(cuts):
        if i:
            copies[i - 1].wait()
        terms[:, start : start + size] = project(hidden, held[0] if i else head, start - ahead if i else 0, scales, start, size)
    width = terms.shape[1]
    for i in range(blocks):
        main, left = pack_all(terms, i, rest, blocks)
        out, at = (outs[0], i) if i < kept else (outs[1], i - kept)
        out[at * TILE : (at + 1) * TILE, :width] = main.astype(out.dtype)
        out[at * TILE : (at + 1) * TILE, width:] = left.astype(out.dtype)


def add_body(mine, other, first, *later):
    first[...] = mine[:TILE, :] + other[:TILE, :].astype(F32)
    for i, ref in enumerate(later):
        rows = slice((i + 1) * TILE, (i + 2) * TILE)
        ref[...] = (mine[rows, :] + other[rows, :].astype(F32)).astype(BF16)


def last_body(*refs):
    out = refs[-1]
    total = refs[0][...]
    for ref in refs[1:-1]:
        total += ref[...].astype(F32)

    def store(row, column, values):
        out[row : row + values.shape[0], column : column + values.shape[1]] = values.astype(out.dtype)

    unpack_rows(total, out.shape[0] - TILE, store)


def rest_space(depth, cuts):
    if len(cuts) == 1:
        return []
    return [pltpu.VMEM((depth, sum(size for _, size in cuts[1:])), BF16), pltpu.SemaphoreType.DMA((len(cuts) - 1,))]


def local(peers, acts, gate_codes, gate_scales, up_codes, up_scales, down_codes, down_scales):
    m, width = acts.shape
    units = gate_codes.shape[1]
    rest = m - TILE
    dense = width + rest * width // TILE
    rows = peers * m
    sds = jax.ShapeDtypeStruct
    pair = peers == 8
    far = peers // 2

    def flip(x):
        return lax.ppermute(x, "hidden", [(h, h ^ 1) for h in range(peers)])

    def along(x, s):
        return lax.ppermute(x, "hidden", [(h, (h + 2 * s) % peers) for h in range(peers)])

    def swap(x):
        return lax.ppermute(x, "width", [(0, 1), (1, 0)])

    def in_vmem(x):
        return pltpu.with_memory_space_constraint(x, pltpu.VMEM)

    packed = call(pack_body, sds((TILE, dense), BF16), [acts], "pack", flops=PACK_WEIGHT)
    if pair:
        line = [packed] + [along(packed, s) for s in range(1, far)]
        blocks = line + [flip(x) for x in line]
    else:
        blocks = [lax.all_gather(packed, "hidden", axis=0, tiled=True)]
    spare = 2 * MIB + 4096 * rows
    up_cuts, down_cuts = pieces(units, 3), pieces(width, 4)
    acts_all, gate, gate_sent, up_head = call(
        functools.partial(gate_body, len(blocks), rest),
        [sds((rows, width), BF16), sds((rows, units), F32), sds((rows, units), BF16), pltpu.VMEM((width, up_cuts[0][1]), BF16)],
        blocks + [in_vmem(gate_codes), gate_scales, up_codes],
        "gate",
        scratch=[pltpu.VMEM((rows, width), F32), pltpu.SemaphoreType.DMA],
        flops=GATE_WEIGHT,
        spare=spare,
        apart=(len(blocks) + 2,),
    )
    gate_other = swap(gate_sent)
    up, up_sent, down_head = call(
        functools.partial(up_body, up_cuts),
        [sds((rows, units), F32), sds((rows, units), BF16), pltpu.VMEM((units, down_cuts[0][1]), BF16)],
        [acts_all, in_vmem(up_head), up_codes, up_scales, down_codes],
        "up",
        scratch=[pltpu.SemaphoreType.DMA] + rest_space(width, up_cuts),
        flops=UP_WEIGHT,
        spare=spare,
        apart=(2, 4),
    )
    up_other = swap(up_sent)
    kept = far if pair else peers
    outs = [sds((kept * TILE, dense), F32)] + ([sds((far * TILE, dense), BF16)] if pair else [])
    parts = call(
        functools.partial(down_body, down_cuts, rest, peers, kept, int(pair)),
        outs,
        [gate, gate_other, up, up_other, in_vmem(down_head), down_codes, down_scales],
        "down",
        scratch=[pltpu.VMEM((rows, units), BF16), pltpu.VMEM((rows, width), F32)] + rest_space(units, down_cuts),
        flops=2 * rows * width * units,
        spare=spare,
        apart=(5,),
    )
    if pair:
        mine, sent = parts
        other = flip(sent)
        sums = call(
            add_body,
            [sds((TILE, dense), F32)] + [sds((TILE, dense), BF16)] * (far - 1),
            [mine, other],
            "add",
        )
        terms = [sums[0]] + [along(x, far - s) for s, x in zip(range(1, far), sums[1:])]
    else:
        terms = [lax.psum_scatter(parts[0], "hidden", scatter_dimension=0, tiled=True)]
    return call(last_body, sds((m, width), BF16), terms, "last")


def solution(mesh):
    placed = (
        P(("replica", "hidden"), "width"),
        P("width", "hidden"),
        P("width", "hidden"),
        P("width", "hidden"),
        P("width", "hidden"),
        P("hidden", "width"),
        P("hidden", "width"),
    )
    return jax.shard_map(
        functools.partial(local, mesh.shape["hidden"]),
        mesh=mesh,
        in_specs=placed,
        out_specs=P(("replica", "hidden"), "width"),
        check_vma=False,
    )
```

```python
import functools
import math

import jax
import jax.numpy as jnp
from jax import lax
from jax.experimental import pallas as pl
from jax.experimental.pallas import tpu as pltpu
from jax.sharding import PartitionSpec as P

BF16, F32 = jnp.bfloat16, jnp.float32
MIB = 1 << 20
PACK_WEIGHT, GATE_WEIGHT, UP_WEIGHT = 60_000_000_000, 10_000_000_000, 10_000_000_000
TILE = 8


def divisor(extent, limit, step):
    for size in range(limit - limit % step, 0, -step):
        if extent % size == 0:
            return size
    return extent


def whole(count):
    return [pl.BlockSpec(memory_space=pltpu.VMEM)] * count


def call(body, out_shape, operands, name, scratch=(), flops=0, apart=(), spare=2 * MIB):
    single = not isinstance(out_shape, list)
    shapes = [out_shape] if single else out_shape
    operands = [pltpu.with_memory_space_constraint(x, pltpu.HBM) if i in apart else x for i, x in enumerate(operands)]
    held = [x for x in scratch if getattr(x, "dtype", None) in (BF16, F32)]
    limit = spare + sum(math.prod(x.shape) * jnp.dtype(x.dtype).itemsize for x in held)
    moved = sum(x.size * x.dtype.itemsize for x in operands)
    return pl.pallas_call(
        body,
        in_specs=[pl.BlockSpec(memory_space=pltpu.HBM if i in apart else pltpu.VMEM) for i in range(len(operands))],
        out_specs=whole(1)[0] if single else whole(len(shapes)),
        out_shape=out_shape,
        scratch_shapes=list(scratch),
        compiler_params=pltpu.CompilerParams(vmem_limit_bytes=limit),
        cost_estimate=pl.CostEstimate(flops=flops, bytes_accessed=moved, transcendentals=0),
        name=name,
    )(*operands)


def pack_body(a_ref, o_ref):
    m, width = a_ref.shape
    rest = m - TILE
    piece = rest * width // TILE
    a = a_ref[...].astype(F32)
    o_ref[:, :width] = a[:TILE].astype(BF16)
    left = [a[TILE:, k * piece : (k + 1) * piece] for k in range(TILE // rest)]
    o_ref[:, width:] = jnp.concatenate(left, axis=0).astype(BF16)


def unpack_rows(block, rest, store):
    width = block.shape[1] * TILE // (TILE + rest)
    piece = rest * width // TILE
    store(0, 0, block[:, :width])
    for k in range(TILE // rest):
        store(TILE, k * piece, block[k * rest : (k + 1) * rest, width:])


def pack_all(total, first, rest, blocks):
    width = total.shape[1]
    piece = rest * width // TILE
    base = blocks * TILE + first * rest
    left = [total[base : base + rest, k * piece : (k + 1) * piece] for k in range(TILE // rest)]
    return total[first * TILE : (first + 1) * TILE, :], jnp.concatenate(left, axis=0)


def dequant(codes, scales):
    depth, width = codes.shape
    groups = scales.shape[0]
    shaped = codes.astype(F32).reshape(groups, depth // groups, width)
    return (shaped * scales[:, None, :]).astype(BF16).reshape(depth, width)


def pieces(width, shares):
    tiles, total = width // 128, sum(shares)
    if width % 128 or tiles < total:
        return [(0, width)]
    ends = [tiles * sum(shares[:k]) // total for k in range(len(shares) + 1)]
    return [(128 * a, 128 * (b - a)) for a, b in zip(ends, ends[1:])]


def project(a_ref, codes_ref, at, scales_ref, start, size):
    depth = codes_ref.shape[0]
    block = depth // scales_ref.shape[0]
    rows = divisor(depth, 512, 8 * block)
    total = jnp.zeros((a_ref.shape[0], size), F32)
    for k in range(0, depth, rows):
        w = dequant(codes_ref[k : k + rows, at : at + size], scales_ref[k // block : (k + rows) // block, start : start + size])
        total += jnp.dot(a_ref[:, k : k + rows], w, preferred_element_type=F32)
    return total


class Copies:
    def __init__(self, *wanted):
        self.waiting, self.started = list(wanted), {}
        self.start()

    def start(self):
        if self.waiting:
            source, start, size, target, at, done = self.waiting.pop(0)
            copy = pltpu.make_async_copy(source.at[:, start : start + size], target.at[:, at : at + size], done)
            copy.start()
            self.started[len(self.started)] = copy

    def wait(self, number):
        while number not in self.started:
            self.start()
        self.started[number].wait()


def gate_body(count, rest, *refs):
    blocks = refs[:count]
    codes, scales, later, acts, own, sent, head, wide, done = refs[count:]
    copy = Copies((later, 0, head.shape[1], head, 0, done))
    total = sum(b.shape[0] for b in blocks) // TILE
    at = 0
    for ref in blocks:
        for i in range(ref.shape[0] // TILE):
            def store(row, column, values):
                first = at * TILE if row == 0 else total * TILE + at * rest
                wide[first : first + values.shape[0], column : column + values.shape[1]] = values
            unpack_rows(ref[i * TILE : (i + 1) * TILE, :].astype(F32), rest, store)
            at += 1
    acts[...] = wide[...].astype(BF16)
    for start, size in pieces(codes.shape[1], (1, 1)):
        total = project(acts, codes, start, scales, start, size)
        own[:, start : start + size] = total
        sent[:, start : start + size] = total.astype(BF16)
    copy.wait(0)


def up_body(cuts, acts, first, codes, scales, later, own, sent, head, done, *tail):
    ahead = first.shape[1]
    ours = [(start, size) for start, size in cuts if start >= ahead]
    wanted = [(codes, start, size, tail[0], start - ahead, done.at[i]) for i, (start, size) in enumerate(ours)]
    copies = Copies(*wanted, (later, 0, head.shape[1], head, 0, done.at[len(ours)]))
    for start, size in cuts:
        if start < ahead:
            total = project(acts, first, start, scales, start, size)
        else:
            copies.wait(ours.index((start, size)))
            total = project(acts, tail[0], start - ahead, scales, start, size)
        copies.start()
        own[:, start : start + size] = total
        sent[:, start : start + size] = total.astype(BF16)
    copies.wait(len(ours))


def emit(terms, blocks, rest, outs):
    width = terms.shape[1]
    kept = outs[0].shape[0] // TILE
    for i in range(blocks):
        main, left = pack_all(terms, i, rest, blocks)
        out, at = (outs[0], i) if i < kept else (outs[1], i - kept)
        out[at * TILE : (at + 1) * TILE, :width] = main.astype(out.dtype)
        out[at * TILE : (at + 1) * TILE, width:] = left.astype(out.dtype)


def first_body(rest, blocks, gate, gate_other, up, up_other, codes, later, scales, *refs):
    *outs, hidden, head, terms, tail, done = refs
    size = codes.shape[1]
    copies = Copies((later, size, size, tail, 0, done.at[0]), (later, 2 * size, size, head, 0, done.at[1]))
    width = divisor(hidden.shape[1], 512, 128)
    for c in range(0, hidden.shape[1], width):
        cols = slice(c, c + width)
        g = gate[:, cols] + gate_other[:, cols].astype(F32)
        u = up[:, cols] + up_other[:, cols].astype(F32)
        hidden[:, cols] = (jax.nn.silu(g) * u).astype(BF16)
    terms[:, :size] = project(hidden, codes, 0, scales, 0, size)
    copies.wait(0)
    copies.start()
    terms[:, size:] = project(hidden, tail, 0, scales, size, size)
    emit(terms, blocks, rest, outs)
    copies.wait(1)


def second_body(rest, blocks, hidden, codes, later, scales, *refs):
    *outs, terms, tail, done = refs
    size = codes.shape[1]
    copies = Copies((later, 3 * size, size, tail, 0, done))
    terms[:, :size] = project(hidden, codes, 0, scales, 2 * size, size)
    copies.wait(0)
    terms[:, size:] = project(hidden, tail, 0, scales, 3 * size, size)
    emit(terms, blocks, rest, outs)


def add_body(count, *refs):
    halves, outs = refs[: 2 * count], refs[2 * count :]
    width = halves[0].shape[1]
    for i, ref in enumerate(outs):
        rows = slice(i * TILE, (i + 1) * TILE)
        for k in range(count):
            total = halves[2 * k][rows, :] + halves[2 * k + 1][rows, :].astype(F32)
            ref[:, k * width : (k + 1) * width] = total.astype(ref.dtype)


def last_body(halves, *refs):
    out = refs[-1]
    total = refs[0][...]
    for ref in refs[1:-1]:
        total += ref[...].astype(F32)
    dense, width = total.shape[1] // halves, out.shape[1] // halves
    for k in range(halves):
        def store(row, column, values):
            column += k * width
            out[row : row + values.shape[0], column : column + values.shape[1]] = values.astype(out.dtype)

        unpack_rows(total[:, k * dense : (k + 1) * dense], out.shape[0] - TILE, store)


def local(peers, acts, gate_codes, gate_scales, up_codes, up_scales, down_codes, down_scales):
    m, width = acts.shape
    units = gate_codes.shape[1]
    rest = m - TILE
    dense = width + rest * width // TILE
    rows = peers * m
    sds = jax.ShapeDtypeStruct
    pair = peers == 8
    far = peers // 2

    def flip(x):
        return lax.ppermute(x, "hidden", [(h, h ^ 1) for h in range(peers)])

    def along(x, s):
        return lax.ppermute(x, "hidden", [(h, (h + 2 * s) % peers) for h in range(peers)])

    def swap(x):
        return lax.ppermute(x, "width", [(0, 1), (1, 0)])

    def in_vmem(x):
        return pltpu.with_memory_space_constraint(x, pltpu.VMEM)

    packed = call(pack_body, sds((TILE, dense), BF16), [acts], "pack", flops=PACK_WEIGHT)
    if pair:
        line = [packed] + [along(packed, s) for s in range(1, far)]
        blocks = line + [flip(x) for x in line]
    else:
        blocks = [lax.all_gather(packed, "hidden", axis=0, tiled=True)]
    spare = 2 * MIB + 4096 * rows
    half, packed_half = width // 2, dense // 2
    quarter = half // 2
    cuts = pieces(units, (1, 1, 1, 1))
    ahead = sum(size for _, size in cuts[:2])
    acts_all, gate, gate_sent, up_head = call(
        functools.partial(gate_body, len(blocks), rest),
        [sds((rows, width), BF16), sds((rows, units), F32), sds((rows, units), BF16), pltpu.VMEM((width, ahead), BF16)],
        blocks + [in_vmem(gate_codes), gate_scales, up_codes],
        "gate",
        scratch=[pltpu.VMEM((rows, width), F32), pltpu.SemaphoreType.DMA],
        flops=GATE_WEIGHT,
        spare=spare,
        apart=(len(blocks) + 2,),
    )
    gate_other = swap(gate_sent)
    tail = [pltpu.VMEM((width, units - ahead), BF16)] if ahead < units else []
    up, up_sent, down_head = call(
        functools.partial(up_body, cuts),
        [sds((rows, units), F32), sds((rows, units), BF16), pltpu.VMEM((units, quarter), BF16)],
        [acts_all, in_vmem(up_head), up_codes, up_scales, down_codes],
        "up",
        scratch=[pltpu.SemaphoreType.DMA((max(len(cuts) - 1, 1),))] + tail,
        flops=UP_WEIGHT,
        spare=spare + 4 * MIB,
        apart=(2, 4),
    )
    up_other = swap(up_sent)
    kept = far if pair else peers
    outs = [sds((kept * TILE, packed_half), F32)] + ([sds((far * TILE, packed_half), BF16)] if pair else [])
    work = rows * width * units
    *first, hidden, down_rest = call(
        functools.partial(first_body, rest, peers),
        outs + [sds((rows, units), BF16), pltpu.VMEM((units, quarter), BF16)],
        [gate, gate_other, up, up_other, in_vmem(down_head), down_codes, down_scales],
        "first",
        scratch=[pltpu.VMEM((rows, half), F32), pltpu.VMEM((units, quarter), BF16), pltpu.SemaphoreType.DMA((2,))],
        flops=work,
        spare=spare,
        apart=(5,),
    )
    if pair:
        first_other = flip(first[1])
    second = call(
        functools.partial(second_body, rest, peers),
        outs,
        [hidden, in_vmem(down_rest), down_codes, down_scales],
        "second",
        scratch=[pltpu.VMEM((rows, half), F32), pltpu.VMEM((units, quarter), BF16), pltpu.SemaphoreType.DMA],
        flops=work,
        spare=spare,
        apart=(2,),
    )
    if pair:
        sums = call(
            functools.partial(add_body, 2),
            [sds((TILE, dense), F32)] + [sds((TILE, dense), BF16)] * (far - 1),
            [first[0], first_other, second[0], flip(second[1])],
            "add",
        )
        terms = [sums[0]] + [along(x, far - s) for s, x in zip(range(1, far), sums[1:])]
    else:
        both = jnp.concatenate([first[0], second[0]], axis=1)
        terms = [lax.psum_scatter(both, "hidden", scatter_dimension=0, tiled=True)]
    return call(functools.partial(last_body, 2), sds((m, width), BF16), terms, "last")


def solution(mesh):
    placed = (
        P(("replica", "hidden"), "width"),
        P("width", "hidden"),
        P("width", "hidden"),
        P("width", "hidden"),
        P("width", "hidden"),
        P("hidden", "width"),
        P("hidden", "width"),
    )
    return jax.shard_map(
        functools.partial(local, mesh.shape["hidden"]),
        mesh=mesh,
        in_specs=placed,
        out_specs=P(("replica", "hidden"), "width"),
        check_vma=False,
    )
```

```python
import functools
import math

import jax
import jax.numpy as jnp
from jax import lax
from jax.experimental import pallas as pl
from jax.experimental.pallas import tpu as pltpu
from jax.sharding import PartitionSpec as P

BF16, F32 = jnp.bfloat16, jnp.float32
MIB = 1 << 20
PACK_WEIGHT, GATE_WEIGHT, UP_WEIGHT = 60_000_000_000, 10_000_000_000, 10_000_000_000
TILE = 8


def divisor(extent, limit, step):
    for size in range(limit - limit % step, 0, -step):
        if extent % size == 0:
            return size
    return extent


def whole(count):
    return [pl.BlockSpec(memory_space=pltpu.VMEM)] * count


def call(body, out_shape, operands, name, scratch=(), flops=0, apart=(), spare=2 * MIB):
    single = not isinstance(out_shape, list)
    shapes = [out_shape] if single else out_shape
    operands = [pltpu.with_memory_space_constraint(x, pltpu.HBM) if i in apart else x for i, x in enumerate(operands)]
    held = [x for x in scratch if getattr(x, "dtype", None) in (BF16, F32)]
    limit = spare + sum(math.prod(x.shape) * jnp.dtype(x.dtype).itemsize for x in held)
    moved = sum(x.size * x.dtype.itemsize for x in operands)
    return pl.pallas_call(
        body,
        in_specs=[pl.BlockSpec(memory_space=pltpu.HBM if i in apart else pltpu.VMEM) for i in range(len(operands))],
        out_specs=whole(1)[0] if single else whole(len(shapes)),
        out_shape=out_shape,
        scratch_shapes=list(scratch),
        compiler_params=pltpu.CompilerParams(vmem_limit_bytes=limit),
        cost_estimate=pl.CostEstimate(flops=flops, bytes_accessed=moved, transcendentals=0),
        name=name,
    )(*operands)


def pack_body(a_ref, o_ref):
    m, width = a_ref.shape
    rest = m - TILE
    piece = rest * width // TILE
    a = a_ref[...].astype(F32)
    o_ref[:, :width] = a[:TILE].astype(BF16)
    left = [a[TILE:, k * piece : (k + 1) * piece] for k in range(TILE // rest)]
    o_ref[:, width:] = jnp.concatenate(left, axis=0).astype(BF16)


def unpack_rows(block, rest, store):
    width = block.shape[1] * TILE // (TILE + rest)
    piece = rest * width // TILE
    store(0, 0, block[:, :width])
    for k in range(TILE // rest):
        store(TILE, k * piece, block[k * rest : (k + 1) * rest, width:])


def pack_all(total, first, rest, blocks):
    width = total.shape[1]
    piece = rest * width // TILE
    base = blocks * TILE + first * rest
    left = [total[base : base + rest, k * piece : (k + 1) * piece] for k in range(TILE // rest)]
    return total[first * TILE : (first + 1) * TILE, :], jnp.concatenate(left, axis=0)


def dequant(codes, scales):
    depth, width = codes.shape
    groups = scales.shape[0]
    spread = jnp.broadcast_to(scales[:, None, :], (groups, depth // groups, width)).astype(BF16)
    return (codes.reshape(groups, depth // groups, width) * spread).reshape(depth, width)


def pieces(width, shares):
    tiles, total = width // 128, sum(shares)
    if width % 128 or tiles < total:
        return [(0, width)]
    ends = [tiles * sum(shares[:k]) // total for k in range(len(shares) + 1)]
    return [(128 * a, 128 * (b - a)) for a, b in zip(ends, ends[1:])]


def project(a_ref, codes_ref, at, scales_ref, start, size):
    depth = codes_ref.shape[0]
    block = depth // scales_ref.shape[0]
    rows = divisor(depth, 512, 8 * block)
    total = jnp.zeros((a_ref.shape[0], size), F32)
    for k in range(0, depth, rows):
        w = dequant(codes_ref[k : k + rows, at : at + size], scales_ref[k // block : (k + rows) // block, start : start + size])
        total += jnp.dot(a_ref[:, k : k + rows], w, preferred_element_type=F32)
    return total


class Copies:
    def __init__(self, *wanted):
        self.waiting, self.started = list(wanted), {}
        self.start()

    def start(self):
        if self.waiting:
            source, start, size, target, at, done = self.waiting.pop(0)
            copy = pltpu.make_async_copy(source.at[:, start : start + size], target.at[:, at : at + size], done)
            copy.start()
            self.started[len(self.started)] = copy

    def wait(self, number):
        while number not in self.started:
            self.start()
        self.started[number].wait()


def gate_body(count, rest, *refs):
    blocks = refs[:count]
    codes, scales, later, acts, own, sent, head, wide, done = refs[count:]
    copy = Copies((later, 0, head.shape[1], head, 0, done))
    total = sum(b.shape[0] for b in blocks) // TILE
    at = 0
    for ref in blocks:
        for i in range(ref.shape[0] // TILE):
            def store(row, column, values):
                first = at * TILE if row == 0 else total * TILE + at * rest
                wide[first : first + values.shape[0], column : column + values.shape[1]] = values
            unpack_rows(ref[i * TILE : (i + 1) * TILE, :].astype(F32), rest, store)
            at += 1
    acts[...] = wide[...].astype(BF16)
    for start, size in pieces(codes.shape[1], (1, 1)):
        total = project(acts, codes, start, scales, start, size)
        own[:, start : start + size] = total
        sent[:, start : start + size] = total.astype(BF16)
    copy.wait(0)


def up_body(cuts, acts, first, codes, scales, later, own, sent, head, done, *tail):
    ahead = first.shape[1]
    ours = [(start, size) for start, size in cuts if start >= ahead]
    wanted = [(codes, start, size, tail[0], start - ahead, done.at[i]) for i, (start, size) in enumerate(ours)]
    copies = Copies(*wanted, (later, 0, head.shape[1], head, 0, done.at[len(ours)]))
    for start, size in cuts:
        if start < ahead:
            total = project(acts, first, start, scales, start, size)
        else:
            copies.wait(ours.index((start, size)))
            total = project(acts, tail[0], start - ahead, scales, start, size)
        copies.start()
        own[:, start : start + size] = total
        sent[:, start : start + size] = total.astype(BF16)
    copies.wait(len(ours))


def emit(terms, blocks, rest, outs):
    width = terms.shape[1]
    kept = outs[0].shape[0] // TILE
    for i in range(blocks):
        main, left = pack_all(terms, i, rest, blocks)
        out, at = (outs[0], i) if i < kept else (outs[1], i - kept)
        out[at * TILE : (at + 1) * TILE, :width] = main.astype(out.dtype)
        out[at * TILE : (at + 1) * TILE, width:] = left.astype(out.dtype)


def first_body(rest, blocks, gate, gate_other, up, up_other, codes, later, scales, *refs):
    *outs, hidden, head, terms, tail, done = refs
    size = codes.shape[1]
    part = size // 2
    copies = Copies(
        (later, size, part, tail, 0, done.at[0]),
        (later, size + part, part, tail, part, done.at[1]),
        (later, 2 * size, size, head, 0, done.at[2]),
    )
    width = divisor(hidden.shape[1], 512, 128)
    for c in range(0, hidden.shape[1], width):
        cols = slice(c, c + width)
        g = gate[:, cols] + gate_other[:, cols].astype(F32)
        u = up[:, cols] + up_other[:, cols].astype(F32)
        hidden[:, cols] = (jax.nn.silu(g) * u).astype(BF16)
    copies.start()
    terms[:, :size] = project(hidden, codes, 0, scales, 0, size)
    copies.start()
    for k in range(2):
        copies.wait(k)
        terms[:, size + k * part : size + (k + 1) * part] = project(hidden, tail, k * part, scales, size + k * part, part)
    emit(terms, blocks, rest, outs)
    copies.wait(2)


def second_body(rest, blocks, hidden, codes, later, scales, *refs):
    *outs, terms, tail, done = refs
    size = codes.shape[1]
    part = size // 2
    copies = Copies(*[(later, 3 * size + k * part, part, tail, k * part, done.at[k]) for k in range(2)])
    for k in range(2):
        terms[:, k * part : (k + 1) * part] = project(hidden, codes, k * part, scales, 2 * size + k * part, part)
        copies.start()
    for k in range(2):
        copies.wait(k)
        terms[:, size + k * part : size + (k + 1) * part] = project(hidden, tail, k * part, scales, 3 * size + k * part, part)
    emit(terms, blocks, rest, outs)


def add_body(count, *refs):
    halves, outs = refs[: 2 * count], refs[2 * count :]
    width = halves[0].shape[1]
    for i, ref in enumerate(outs):
        rows = slice(i * TILE, (i + 1) * TILE)
        for k in range(count):
            total = halves[2 * k][rows, :] + halves[2 * k + 1][rows, :].astype(F32)
            ref[:, k * width : (k + 1) * width] = total.astype(ref.dtype)


def last_body(halves, *refs):
    out = refs[-1]
    total = refs[0][...]
    for ref in refs[1:-1]:
        total += ref[...].astype(F32)
    dense, width = total.shape[1] // halves, out.shape[1] // halves
    for k in range(halves):
        def store(row, column, values):
            column += k * width
            out[row : row + values.shape[0], column : column + values.shape[1]] = values.astype(out.dtype)

        unpack_rows(total[:, k * dense : (k + 1) * dense], out.shape[0] - TILE, store)


def local(peers, acts, gate_codes, gate_scales, up_codes, up_scales, down_codes, down_scales):
    m, width = acts.shape
    units = gate_codes.shape[1]
    rest = m - TILE
    dense = width + rest * width // TILE
    rows = peers * m
    sds = jax.ShapeDtypeStruct
    pair = peers == 8
    far = peers // 2

    def flip(x):
        return lax.ppermute(x, "hidden", [(h, h ^ 1) for h in range(peers)])

    def along(x, s):
        return lax.ppermute(x, "hidden", [(h, (h + 2 * s) % peers) for h in range(peers)])

    def swap(x):
        return lax.ppermute(x, "width", [(0, 1), (1, 0)])

    def in_vmem(x):
        return pltpu.with_memory_space_constraint(x, pltpu.VMEM)

    packed = call(pack_body, sds((TILE, dense), BF16), [acts], "pack", flops=PACK_WEIGHT)
    if pair:
        line = [packed] + [along(packed, s) for s in range(1, far)]
        blocks = line + [flip(x) for x in line]
    else:
        blocks = [lax.all_gather(packed, "hidden", axis=0, tiled=True)]
    spare = 2 * MIB + 4096 * rows
    half, packed_half = width // 2, dense // 2
    quarter = half // 2
    cuts = pieces(units, (1, 1, 1, 1))
    ahead = sum(size for _, size in cuts[:2])
    acts_all, gate, gate_sent, up_head = call(
        functools.partial(gate_body, len(blocks), rest),
        [sds((rows, width), BF16), sds((rows, units), F32), sds((rows, units), BF16), pltpu.VMEM((width, ahead), BF16)],
        blocks + [in_vmem(gate_codes), gate_scales, up_codes],
        "gate",
        scratch=[pltpu.VMEM((rows, width), F32), pltpu.SemaphoreType.DMA],
        flops=GATE_WEIGHT,
        spare=spare,
        apart=(len(blocks) + 2,),
    )
    gate_other = swap(gate_sent)
    tail = [pltpu.VMEM((width, units - ahead), BF16)] if ahead < units else []
    up, up_sent, down_head = call(
        functools.partial(up_body, cuts),
        [sds((rows, units), F32), sds((rows, units), BF16), pltpu.VMEM((units, quarter), BF16)],
        [acts_all, in_vmem(up_head), up_codes, up_scales, down_codes],
        "up",
        scratch=[pltpu.SemaphoreType.DMA((max(len(cuts) - 1, 1),))] + tail,
        flops=UP_WEIGHT,
        spare=spare + 4 * MIB,
        apart=(2, 4),
    )
    up_other = swap(up_sent)
    kept = far if pair else peers
    outs = [sds((kept * TILE, packed_half), F32)] + ([sds((far * TILE, packed_half), BF16)] if pair else [])
    work = rows * width * units
    *first, hidden, down_rest = call(
        functools.partial(first_body, rest, peers),
        outs + [sds((rows, units), BF16), pltpu.VMEM((units, quarter), BF16)],
        [gate, gate_other, up, up_other, in_vmem(down_head), down_codes, down_scales],
        "first",
        scratch=[pltpu.VMEM((rows, half), F32), pltpu.VMEM((units, quarter), BF16), pltpu.SemaphoreType.DMA((3,))],
        flops=work,
        spare=spare,
        apart=(5,),
    )
    if pair:
        first_other = flip(first[1])
    second = call(
        functools.partial(second_body, rest, peers),
        outs,
        [hidden, in_vmem(down_rest), down_codes, down_scales],
        "second",
        scratch=[pltpu.VMEM((rows, half), F32), pltpu.VMEM((units, quarter), BF16), pltpu.SemaphoreType.DMA((2,))],
        flops=work,
        spare=spare,
        apart=(2,),
    )
    if pair:
        sums = call(
            functools.partial(add_body, 2),
            [sds((TILE, dense), F32)] + [sds((TILE, dense), BF16)] * (far - 1),
            [first[0], first_other, second[0], flip(second[1])],
            "add",
        )
        terms = [sums[0]] + [along(x, far - s) for s, x in zip(range(1, far), sums[1:])]
    else:
        both = jnp.concatenate([first[0], second[0]], axis=1)
        terms = [lax.psum_scatter(both, "hidden", scatter_dimension=0, tiled=True)]
    return call(functools.partial(last_body, 2), sds((m, width), BF16), terms, "last")


def solution(mesh):
    placed = (
        P(("replica", "hidden"), "width"),
        P("width", "hidden"),
        P("width", "hidden"),
        P("width", "hidden"),
        P("width", "hidden"),
        P("hidden", "width"),
        P("hidden", "width"),
    )
    return jax.shard_map(
        functools.partial(local, mesh.shape["hidden"]),
        mesh=mesh,
        in_specs=placed,
        out_specs=P(("replica", "hidden"), "width"),
        check_vma=False,
    )
```

```python
import functools
import math

import jax
import jax.numpy as jnp
from jax import lax
from jax.experimental import pallas as pl
from jax.experimental.pallas import tpu as pltpu
from jax.sharding import PartitionSpec as P

BF16, F32 = jnp.bfloat16, jnp.float32
MIB = 1 << 20
PACK_WEIGHT, GATE_WEIGHT, UP_WEIGHT = 60_000_000_000, 10_000_000_000, 10_000_000_000
TILE = 8


def divisor(extent, limit, step):
    for size in range(limit - limit % step, 0, -step):
        if extent % size == 0:
            return size
    return extent


def whole(count):
    return [pl.BlockSpec(memory_space=pltpu.VMEM)] * count


def call(body, out_shape, operands, name, scratch=(), flops=0, apart=(), spare=2 * MIB):
    single = not isinstance(out_shape, list)
    shapes = [out_shape] if single else out_shape
    operands = [pltpu.with_memory_space_constraint(x, pltpu.HBM) if i in apart else x for i, x in enumerate(operands)]
    held = [x for x in scratch if getattr(x, "dtype", None) in (BF16, F32)]
    limit = spare + sum(math.prod(x.shape) * jnp.dtype(x.dtype).itemsize for x in held)
    moved = sum(x.size * x.dtype.itemsize for x in operands)
    return pl.pallas_call(
        body,
        in_specs=[pl.BlockSpec(memory_space=pltpu.HBM if i in apart else pltpu.VMEM) for i in range(len(operands))],
        out_specs=whole(1)[0] if single else whole(len(shapes)),
        out_shape=out_shape,
        scratch_shapes=list(scratch),
        compiler_params=pltpu.CompilerParams(vmem_limit_bytes=limit),
        cost_estimate=pl.CostEstimate(flops=flops, bytes_accessed=moved, transcendentals=0),
        name=name,
    )(*operands)


def pack_body(a_ref, o_ref):
    m, width = a_ref.shape
    rest = m - TILE
    piece = rest * width // TILE
    a = a_ref[...].astype(F32)
    o_ref[:, :width] = a[:TILE].astype(BF16)
    left = [a[TILE:, k * piece : (k + 1) * piece] for k in range(TILE // rest)]
    o_ref[:, width:] = jnp.concatenate(left, axis=0).astype(BF16)


def unpack_rows(block, rest, store):
    width = block.shape[1] * TILE // (TILE + rest)
    piece = rest * width // TILE
    store(0, 0, block[:, :width])
    for k in range(TILE // rest):
        store(TILE, k * piece, block[k * rest : (k + 1) * rest, width:])


def pack_all(total, first, rest, blocks):
    width = total.shape[1]
    piece = rest * width // TILE
    base = blocks * TILE + first * rest
    left = [total[base : base + rest, k * piece : (k + 1) * piece] for k in range(TILE // rest)]
    return total[first * TILE : (first + 1) * TILE, :], jnp.concatenate(left, axis=0)


def dequant_short(codes, scales):
    depth, width = codes.shape
    groups = scales.shape[0]
    spread = jnp.broadcast_to(scales[:, None, :], (groups, depth // groups, width)).astype(BF16)
    return (codes.reshape(groups, depth // groups, width) * spread).reshape(depth, width)


def dequant(codes, scales):
    depth, width = codes.shape
    groups = scales.shape[0]
    shaped = codes.astype(F32).reshape(groups, depth // groups, width)
    return (shaped * scales[:, None, :]).astype(BF16).reshape(depth, width)


def pieces(width, shares):
    tiles, total = width // 128, sum(shares)
    if width % 128 or tiles < total:
        return [(0, width)]
    ends = [tiles * sum(shares[:k]) // total for k in range(len(shares) + 1)]
    return [(128 * a, 128 * (b - a)) for a, b in zip(ends, ends[1:])]


def project(a_ref, codes_ref, at, scales_ref, start, size, product=dequant):
    depth = codes_ref.shape[0]
    block = depth // scales_ref.shape[0]
    rows = divisor(depth, 512, 8 * block)
    total = jnp.zeros((a_ref.shape[0], size), F32)
    for k in range(0, depth, rows):
        w = product(codes_ref[k : k + rows, at : at + size], scales_ref[k // block : (k + rows) // block, start : start + size])
        total += jnp.dot(a_ref[:, k : k + rows], w, preferred_element_type=F32)
    return total


class Copies:
    def __init__(self, *wanted):
        self.waiting, self.started = list(wanted), {}
        self.start()

    def start(self):
        if self.waiting:
            source, start, size, target, at, done = self.waiting.pop(0)
            copy = pltpu.make_async_copy(source.at[:, start : start + size], target.at[:, at : at + size], done)
            copy.start()
            self.started[len(self.started)] = copy

    def wait(self, number):
        while number not in self.started:
            self.start()
        self.started[number].wait()


def gate_body(count, rest, *refs):
    blocks = refs[:count]
    codes, scales, later, acts, own, sent, head, wide, done = refs[count:]
    copy = Copies((later, 0, head.shape[1], head, 0, done))
    total = sum(b.shape[0] for b in blocks) // TILE
    at = 0
    for ref in blocks:
        for i in range(ref.shape[0] // TILE):
            def store(row, column, values):
                first = at * TILE if row == 0 else total * TILE + at * rest
                wide[first : first + values.shape[0], column : column + values.shape[1]] = values
            unpack_rows(ref[i * TILE : (i + 1) * TILE, :].astype(F32), rest, store)
            at += 1
    acts[...] = wide[...].astype(BF16)
    for start, size in pieces(codes.shape[1], (1, 1)):
        total = project(acts, codes, start, scales, start, size, dequant_short)
        own[:, start : start + size] = total
        sent[:, start : start + size] = total.astype(BF16)
    copy.wait(0)


def up_body(cuts, acts, first, codes, scales, later, own, sent, head, done, *tail):
    ahead = first.shape[1]
    ours = [(start, size) for start, size in cuts if start >= ahead]
    wanted = [(codes, start, size, tail[0], start - ahead, done.at[i]) for i, (start, size) in enumerate(ours)]
    copies = Copies(*wanted, (later, 0, head.shape[1], head, 0, done.at[len(ours)]))
    for start, size in cuts:
        if start < ahead:
            total = project(acts, first, start, scales, start, size)
        else:
            copies.wait(ours.index((start, size)))
            total = project(acts, tail[0], start - ahead, scales, start, size)
        copies.start()
        own[:, start : start + size] = total
        sent[:, start : start + size] = total.astype(BF16)
    copies.wait(len(ours))


def emit(terms, blocks, rest, outs):
    width = terms.shape[1]
    kept = outs[0].shape[0] // TILE
    for i in range(blocks):
        main, left = pack_all(terms, i, rest, blocks)
        out, at = (outs[0], i) if i < kept else (outs[1], i - kept)
        out[at * TILE : (at + 1) * TILE, :width] = main.astype(out.dtype)
        out[at * TILE : (at + 1) * TILE, width:] = left.astype(out.dtype)


def first_body(rest, blocks, gate, gate_other, up, up_other, codes, later, scales, *refs):
    *outs, hidden, head, terms, tail, done = refs
    size = codes.shape[1]
    part = size // 2
    copies = Copies(
        (later, size, part, tail, 0, done.at[0]),
        (later, size + part, part, tail, part, done.at[1]),
        (later, 2 * size, size, head, 0, done.at[2]),
    )
    width = divisor(hidden.shape[1], 512, 128)
    for c in range(0, hidden.shape[1], width):
        cols = slice(c, c + width)
        g = gate[:, cols] + gate_other[:, cols].astype(F32)
        u = up[:, cols] + up_other[:, cols].astype(F32)
        hidden[:, cols] = (jax.nn.silu(g) * u).astype(BF16)
    copies.start()
    terms[:, :size] = project(hidden, codes, 0, scales, 0, size)
    copies.start()
    for k in range(2):
        copies.wait(k)
        terms[:, size + k * part : size + (k + 1) * part] = project(hidden, tail, k * part, scales, size + k * part, part)
    emit(terms, blocks, rest, outs)
    copies.wait(2)


def second_body(rest, blocks, hidden, codes, later, scales, *refs):
    *outs, terms, tail, done = refs
    size = codes.shape[1]
    part = size // 2
    copies = Copies(*[(later, 3 * size + k * part, part, tail, k * part, done.at[k]) for k in range(2)])
    for k in range(2):
        terms[:, k * part : (k + 1) * part] = project(hidden, codes, k * part, scales, 2 * size + k * part, part)
        copies.start()
    for k in range(2):
        copies.wait(k)
        terms[:, size + k * part : size + (k + 1) * part] = project(hidden, tail, k * part, scales, 3 * size + k * part, part)
    emit(terms, blocks, rest, outs)


def add_body(count, *refs):
    halves, outs = refs[: 2 * count], refs[2 * count :]
    width = halves[0].shape[1]
    for i, ref in enumerate(outs):
        rows = slice(i * TILE, (i + 1) * TILE)
        for k in range(count):
            total = halves[2 * k][rows, :] + halves[2 * k + 1][rows, :].astype(F32)
            ref[:, k * width : (k + 1) * width] = total.astype(ref.dtype)


def last_body(halves, *refs):
    out = refs[-1]
    total = refs[0][...]
    for ref in refs[1:-1]:
        total += ref[...].astype(F32)
    dense, width = total.shape[1] // halves, out.shape[1] // halves
    for k in range(halves):
        def store(row, column, values):
            column += k * width
            out[row : row + values.shape[0], column : column + values.shape[1]] = values.astype(out.dtype)

        unpack_rows(total[:, k * dense : (k + 1) * dense], out.shape[0] - TILE, store)


def local(peers, acts, gate_codes, gate_scales, up_codes, up_scales, down_codes, down_scales):
    m, width = acts.shape
    units = gate_codes.shape[1]
    rest = m - TILE
    dense = width + rest * width // TILE
    rows = peers * m
    sds = jax.ShapeDtypeStruct
    pair = peers == 8
    far = peers // 2

    def flip(x):
        return lax.ppermute(x, "hidden", [(h, h ^ 1) for h in range(peers)])

    def along(x, s):
        return lax.ppermute(x, "hidden", [(h, (h + 2 * s) % peers) for h in range(peers)])

    def swap(x):
        return lax.ppermute(x, "width", [(0, 1), (1, 0)])

    def in_vmem(x):
        return pltpu.with_memory_space_constraint(x, pltpu.VMEM)

    packed = call(pack_body, sds((TILE, dense), BF16), [acts], "pack", flops=PACK_WEIGHT)
    if pair:
        line = [packed] + [along(packed, s) for s in range(1, far)]
        across = flip(packed)
        blocks = line + [across] + [along(across, s) if s == 2 else flip(line[s]) for s in range(1, far)]
    else:
        blocks = [lax.all_gather(packed, "hidden", axis=0, tiled=True)]
    spare = 2 * MIB + 4096 * rows
    half, packed_half = width // 2, dense // 2
    quarter = half // 2
    cuts = pieces(units, (1, 1, 1, 1))
    ahead = sum(size for _, size in cuts[:2])
    acts_all, gate, gate_sent, up_head = call(
        functools.partial(gate_body, len(blocks), rest),
        [sds((rows, width), BF16), sds((rows, units), F32), sds((rows, units), BF16), pltpu.VMEM((width, ahead), BF16)],
        blocks + [in_vmem(gate_codes), gate_scales, up_codes],
        "gate",
        scratch=[pltpu.VMEM((rows, width), F32), pltpu.SemaphoreType.DMA],
        flops=GATE_WEIGHT,
        spare=spare,
        apart=(len(blocks) + 2,),
    )
    gate_other = swap(gate_sent)
    tail = [pltpu.VMEM((width, units - ahead), BF16)] if ahead < units else []
    up, up_sent, down_head = call(
        functools.partial(up_body, cuts),
        [sds((rows, units), F32), sds((rows, units), BF16), pltpu.VMEM((units, quarter), BF16)],
        [acts_all, in_vmem(up_head), up_codes, up_scales, down_codes],
        "up",
        scratch=[pltpu.SemaphoreType.DMA((max(len(cuts) - 1, 1),))] + tail,
        flops=UP_WEIGHT,
        spare=spare + 4 * MIB,
        apart=(2, 4),
    )
    up_other = swap(up_sent)
    kept = far if pair else peers
    outs = [sds((kept * TILE, packed_half), F32)] + ([sds((far * TILE, packed_half), BF16)] if pair else [])
    work = rows * width * units
    *first, hidden, down_rest = call(
        functools.partial(first_body, rest, peers),
        outs + [sds((rows, units), BF16), pltpu.VMEM((units, quarter), BF16)],
        [gate, gate_other, up, up_other, in_vmem(down_head), down_codes, down_scales],
        "first",
        scratch=[pltpu.VMEM((rows, half), F32), pltpu.VMEM((units, quarter), BF16), pltpu.SemaphoreType.DMA((3,))],
        flops=work,
        spare=spare,
        apart=(5,),
    )
    if pair:
        first_other = flip(first[1])
    second = call(
        functools.partial(second_body, rest, peers),
        outs,
        [hidden, in_vmem(down_rest), down_codes, down_scales],
        "second",
        scratch=[pltpu.VMEM((rows, half), F32), pltpu.VMEM((units, quarter), BF16), pltpu.SemaphoreType.DMA((2,))],
        flops=work,
        spare=spare,
        apart=(2,),
    )
    if pair:
        sums = call(
            functools.partial(add_body, 2),
            [sds((TILE, dense), F32)] + [sds((TILE, dense), BF16)] * (far - 1),
            [first[0], first_other, second[0], flip(second[1])],
            "add",
        )
        terms = [sums[0]] + [along(x, far - s) for s, x in zip(range(1, far), sums[1:])]
    else:
        both = jnp.concatenate([first[0], second[0]], axis=1)
        terms = [lax.psum_scatter(both, "hidden", scatter_dimension=0, tiled=True)]
    return call(functools.partial(last_body, 2), sds((m, width), BF16), terms, "last")


def solution(mesh):
    placed = (
        P(("replica", "hidden"), "width"),
        P("width", "hidden"),
        P("width", "hidden"),
        P("width", "hidden"),
        P("width", "hidden"),
        P("hidden", "width"),
        P("hidden", "width"),
    )
    return jax.shard_map(
        functools.partial(local, mesh.shape["hidden"]),
        mesh=mesh,
        in_specs=placed,
        out_specs=P(("replica", "hidden"), "width"),
        check_vma=False,
    )
```

```python
import functools
import math

import jax
import jax.numpy as jnp
from jax import lax
from jax.experimental import pallas as pl
from jax.experimental.pallas import tpu as pltpu
from jax.sharding import PartitionSpec as P

BF16, F32 = jnp.bfloat16, jnp.float32
MIB = 1 << 20
PACK_WEIGHT, GATE_WEIGHT, UP_WEIGHT = 60_000_000_000, 10_000_000_000, 10_000_000_000
TILE = 8


def divisor(extent, limit, step):
    for size in range(limit - limit % step, 0, -step):
        if extent % size == 0:
            return size
    return extent


def whole(count):
    return [pl.BlockSpec(memory_space=pltpu.VMEM)] * count


def call(body, out_shape, operands, name, scratch=(), flops=0, apart=(), spare=2 * MIB):
    single = not isinstance(out_shape, list)
    shapes = [out_shape] if single else out_shape
    operands = [pltpu.with_memory_space_constraint(x, pltpu.HBM) if i in apart else x for i, x in enumerate(operands)]
    held = [x for x in scratch if getattr(x, "dtype", None) in (BF16, F32)]
    limit = spare + sum(math.prod(x.shape) * jnp.dtype(x.dtype).itemsize for x in held)
    moved = sum(x.size * x.dtype.itemsize for x in operands)
    return pl.pallas_call(
        body,
        in_specs=[pl.BlockSpec(memory_space=pltpu.HBM if i in apart else pltpu.VMEM) for i in range(len(operands))],
        out_specs=whole(1)[0] if single else whole(len(shapes)),
        out_shape=out_shape,
        scratch_shapes=list(scratch),
        compiler_params=pltpu.CompilerParams(vmem_limit_bytes=limit),
        cost_estimate=pl.CostEstimate(flops=flops, bytes_accessed=moved, transcendentals=0),
        name=name,
    )(*operands)


def pack_body(a_ref, o_ref):
    m, width = a_ref.shape
    rest = m - TILE
    piece = rest * width // TILE
    a = a_ref[...].astype(F32)
    o_ref[:, :width] = a[:TILE].astype(BF16)
    left = [a[TILE:, k * piece : (k + 1) * piece] for k in range(TILE // rest)]
    o_ref[:, width:] = jnp.concatenate(left, axis=0).astype(BF16)


def unpack_rows(block, rest, store):
    width = block.shape[1] * TILE // (TILE + rest)
    piece = rest * width // TILE
    store(0, 0, block[:, :width])
    for k in range(TILE // rest):
        store(TILE, k * piece, block[k * rest : (k + 1) * rest, width:])


def pack_all(total, first, rest, blocks):
    width = total.shape[1]
    piece = rest * width // TILE
    base = blocks * TILE + first * rest
    left = [total[base : base + rest, k * piece : (k + 1) * piece] for k in range(TILE // rest)]
    return total[first * TILE : (first + 1) * TILE, :], jnp.concatenate(left, axis=0)


def dequant_short(codes, scales):
    depth, width = codes.shape
    groups = scales.shape[0]
    spread = jnp.broadcast_to(scales[:, None, :], (groups, depth // groups, width)).astype(BF16)
    return (codes.reshape(groups, depth // groups, width) * spread).reshape(depth, width)


def dequant(codes, scales):
    depth, width = codes.shape
    groups = scales.shape[0]
    shaped = codes.astype(F32).reshape(groups, depth // groups, width)
    return (shaped * scales[:, None, :]).astype(BF16).reshape(depth, width)


def pieces(width, shares):
    tiles, total = width // 128, sum(shares)
    if width % 128 or tiles < total:
        return [(0, width)]
    ends = [tiles * sum(shares[:k]) // total for k in range(len(shares) + 1)]
    return [(128 * a, 128 * (b - a)) for a, b in zip(ends, ends[1:])]


def project(a_ref, codes_ref, at, scales_ref, start, size, product=dequant):
    depth = codes_ref.shape[0]
    block = depth // scales_ref.shape[0]
    rows = divisor(depth, 512, 8 * block)
    total = jnp.zeros((a_ref.shape[0], size), F32)
    for k in range(0, depth, rows):
        w = product(codes_ref[k : k + rows, at : at + size], scales_ref[k // block : (k + rows) // block, start : start + size])
        total += jnp.dot(a_ref[:, k : k + rows], w, preferred_element_type=F32)
    return total


class Copies:
    def __init__(self, *wanted):
        self.waiting, self.started = list(wanted), {}
        self.start()

    def start(self):
        if self.waiting:
            source, start, size, target, at, done = self.waiting.pop(0)
            copy = pltpu.make_async_copy(source.at[:, start : start + size], target.at[:, at : at + size], done)
            copy.start()
            self.started[len(self.started)] = copy

    def wait(self, number):
        while number not in self.started:
            self.start()
        self.started[number].wait()


def gate_body(count, rest, *refs):
    blocks = refs[:count]
    codes, scales, later, acts, own, sent, head, wide, done = refs[count:]
    copy = Copies((later, 0, head.shape[1], head, 0, done))
    total = sum(b.shape[0] for b in blocks) // TILE
    at = 0
    for ref in blocks:
        for i in range(ref.shape[0] // TILE):
            def store(row, column, values):
                first = at * TILE if row == 0 else total * TILE + at * rest
                wide[first : first + values.shape[0], column : column + values.shape[1]] = values
            unpack_rows(ref[i * TILE : (i + 1) * TILE, :].astype(F32), rest, store)
            at += 1
    acts[...] = wide[...].astype(BF16)
    for start, size in pieces(codes.shape[1], (1, 1)):
        total = project(acts, codes, start, scales, start, size, dequant_short)
        own[:, start : start + size] = total
        sent[:, start : start + size] = total.astype(BF16)
    copy.wait(0)


def up_body(cuts, acts, first, codes, scales, later, own, sent, head, done, *tail):
    ahead = first.shape[1]
    ours = [(start, size) for start, size in cuts if start >= ahead]
    wanted = [(codes, start, size, tail[0], start - ahead, done.at[i]) for i, (start, size) in enumerate(ours)]
    copies = Copies(*wanted, (later, 0, head.shape[1], head, 0, done.at[len(ours)]))
    for start, size in cuts:
        if start < ahead:
            total = project(acts, first, start, scales, start, size)
        else:
            copies.wait(ours.index((start, size)))
            total = project(acts, tail[0], start - ahead, scales, start, size)
        copies.start()
        own[:, start : start + size] = total
        sent[:, start : start + size] = total.astype(BF16)
    copies.wait(len(ours))


def emit(terms, blocks, rest, outs):
    width = terms.shape[1]
    kept = outs[0].shape[0] // TILE
    for i in range(blocks):
        main, left = pack_all(terms, i, rest, blocks)
        out, at = (outs[0], i) if i < kept else (outs[1], i - kept)
        out[at * TILE : (at + 1) * TILE, :width] = main.astype(out.dtype)
        out[at * TILE : (at + 1) * TILE, width:] = left.astype(out.dtype)


def first_body(rest, blocks, gate, gate_other, up, up_other, codes, later, scales, *refs):
    *outs, hidden, head, terms, tail, done = refs
    size = codes.shape[1]
    part = size // 2
    copies = Copies(
        (later, size, part, tail, 0, done.at[0]),
        (later, size + part, part, tail, part, done.at[1]),
        (later, 2 * size, size, head, 0, done.at[2]),
    )
    width = divisor(hidden.shape[1], 512, 128)
    for c in range(0, hidden.shape[1], width):
        cols = slice(c, c + width)
        g = gate[:, cols] + gate_other[:, cols].astype(F32)
        u = up[:, cols] + up_other[:, cols].astype(F32)
        hidden[:, cols] = (jax.nn.silu(g) * u).astype(BF16)
    copies.start()
    terms[:, :size] = project(hidden, codes, 0, scales, 0, size)
    copies.start()
    for k in range(2):
        copies.wait(k)
        terms[:, size + k * part : size + (k + 1) * part] = project(hidden, tail, k * part, scales, size + k * part, part)
    emit(terms, blocks, rest, outs)
    copies.wait(2)


def second_body(rest, blocks, hidden, codes, later, scales, *refs):
    *outs, terms, tail, done = refs
    size = codes.shape[1]
    part = size // 2
    copies = Copies(*[(later, 3 * size + k * part, part, tail, k * part, done.at[k]) for k in range(2)])
    for k in range(2):
        terms[:, k * part : (k + 1) * part] = project(hidden, codes, k * part, scales, 2 * size + k * part, part)
        copies.start()
    for k in range(2):
        copies.wait(k)
        terms[:, size + k * part : size + (k + 1) * part] = project(hidden, tail, k * part, scales, 3 * size + k * part, part)
    emit(terms, blocks, rest, outs)


def add_body(count, *refs):
    halves, outs = refs[: 2 * count], refs[2 * count :]
    width = halves[0].shape[1]
    for i, ref in enumerate(outs):
        rows = slice(i * TILE, (i + 1) * TILE)
        for k in range(count):
            total = halves[2 * k][rows, :] + halves[2 * k + 1][rows, :].astype(F32)
            ref[:, k * width : (k + 1) * width] = total.astype(ref.dtype)


def last_body(halves, *refs):
    out, count = refs[-1], len(refs) // halves
    width = out.shape[1] // halves
    for k in range(halves):
        terms = refs[k * count : (k + 1) * count]
        total = terms[0][...]
        for ref in terms[1:]:
            total += ref[...].astype(F32)

        def store(row, column, values):
            column += k * width
            out[row : row + values.shape[0], column : column + values.shape[1]] = values.astype(out.dtype)

        unpack_rows(total, out.shape[0] - TILE, store)


def local(peers, acts, gate_codes, gate_scales, up_codes, up_scales, down_codes, down_scales):
    m, width = acts.shape
    units = gate_codes.shape[1]
    rest = m - TILE
    dense = width + rest * width // TILE
    rows = peers * m
    sds = jax.ShapeDtypeStruct
    pair = peers == 8
    far = peers // 2

    def flip(x):
        return lax.ppermute(x, "hidden", [(h, h ^ 1) for h in range(peers)])

    def along(x, s):
        return lax.ppermute(x, "hidden", [(h, (h + 2 * s) % peers) for h in range(peers)])

    def swap(x):
        return lax.ppermute(x, "width", [(0, 1), (1, 0)])

    def in_vmem(x):
        return pltpu.with_memory_space_constraint(x, pltpu.VMEM)

    packed = call(pack_body, sds((TILE, dense), BF16), [acts], "pack", flops=PACK_WEIGHT)
    if pair:
        line = [packed] + [along(packed, s) for s in range(1, far)]
        across = flip(packed)
        blocks = line + [across] + [along(across, s) if s == 2 else flip(line[s]) for s in range(1, far)]
    else:
        blocks = [lax.all_gather(packed, "hidden", axis=0, tiled=True)]
    spare = 2 * MIB + 4096 * rows
    half, packed_half = width // 2, dense // 2
    quarter = half // 2
    cuts = pieces(units, (1, 1, 1, 1))
    ahead = sum(size for _, size in cuts[:2])
    acts_all, gate, gate_sent, up_head = call(
        functools.partial(gate_body, len(blocks), rest),
        [sds((rows, width), BF16), sds((rows, units), F32), sds((rows, units), BF16), pltpu.VMEM((width, ahead), BF16)],
        blocks + [in_vmem(gate_codes), gate_scales, up_codes],
        "gate",
        scratch=[pltpu.VMEM((rows, width), F32), pltpu.SemaphoreType.DMA],
        flops=GATE_WEIGHT,
        spare=spare,
        apart=(len(blocks) + 2,),
    )
    gate_other = swap(gate_sent)
    tail = [pltpu.VMEM((width, units - ahead), BF16)] if ahead < units else []
    up, up_sent, down_head = call(
        functools.partial(up_body, cuts),
        [sds((rows, units), F32), sds((rows, units), BF16), pltpu.VMEM((units, quarter), BF16)],
        [acts_all, in_vmem(up_head), up_codes, up_scales, down_codes],
        "up",
        scratch=[pltpu.SemaphoreType.DMA((max(len(cuts) - 1, 1),))] + tail,
        flops=UP_WEIGHT,
        spare=spare + 4 * MIB,
        apart=(2, 4),
    )
    up_other = swap(up_sent)
    kept = far if pair else peers
    outs = [sds((kept * TILE, packed_half), F32)] + ([sds((far * TILE, packed_half), BF16)] if pair else [])
    work = rows * width * units
    *first, hidden, down_rest = call(
        functools.partial(first_body, rest, peers),
        outs + [sds((rows, units), BF16), pltpu.VMEM((units, quarter), BF16)],
        [gate, gate_other, up, up_other, in_vmem(down_head), down_codes, down_scales],
        "first",
        scratch=[pltpu.VMEM((rows, half), F32), pltpu.VMEM((units, quarter), BF16), pltpu.SemaphoreType.DMA((3,))],
        flops=work,
        spare=spare,
        apart=(5,),
    )
    if pair:
        first_other = flip(first[1])
    second = call(
        functools.partial(second_body, rest, peers),
        outs,
        [hidden, in_vmem(down_rest), down_codes, down_scales],
        "second",
        scratch=[pltpu.VMEM((rows, half), F32), pltpu.VMEM((units, quarter), BF16), pltpu.SemaphoreType.DMA((2,))],
        flops=work,
        spare=spare,
        apart=(2,),
    )
    if pair:
        terms = []
        for mine, other in ((first[0], first_other), (second[0], flip(second[1]))):
            sums = call(
                functools.partial(add_body, 1),
                [sds((TILE, packed_half), F32)] + [sds((TILE, packed_half), BF16)] * (far - 1),
                [mine, other],
                "add",
            )
            terms += [sums[0]] + [along(x, far - s) for s, x in zip(range(1, far), sums[1:])]
    else:
        both = [lax.psum_scatter(x[0], "hidden", scatter_dimension=0, tiled=True) for x in (first, second)]
        terms = both
    return call(functools.partial(last_body, 2), sds((m, width), BF16), terms, "last")


def solution(mesh):
    placed = (
        P(("replica", "hidden"), "width"),
        P("width", "hidden"),
        P("width", "hidden"),
        P("width", "hidden"),
        P("width", "hidden"),
        P("hidden", "width"),
        P("hidden", "width"),
    )
    return jax.shard_map(
        functools.partial(local, mesh.shape["hidden"]),
        mesh=mesh,
        in_specs=placed,
        out_specs=P(("replica", "hidden"), "width"),
        check_vma=False,
    )
```

```python
import functools
import math

import jax
import jax.numpy as jnp
from jax import lax
from jax.experimental import pallas as pl
from jax.experimental.pallas import tpu as pltpu
from jax.sharding import PartitionSpec as P

BF16, F32 = jnp.bfloat16, jnp.float32
MIB = 1 << 20
PACK_WEIGHT, GATE_WEIGHT, UP_WEIGHT = 60_000_000_000, 10_000_000_000, 10_000_000_000
TILE = 8


def divisor(extent, limit, step):
    for size in range(limit - limit % step, 0, -step):
        if extent % size == 0:
            return size
    return extent


def whole(count):
    return [pl.BlockSpec(memory_space=pltpu.VMEM)] * count


def call(body, out_shape, operands, name, scratch=(), flops=0, apart=(), spare=2 * MIB):
    single = not isinstance(out_shape, list)
    shapes = [out_shape] if single else out_shape
    operands = [pltpu.with_memory_space_constraint(x, pltpu.HBM) if i in apart else x for i, x in enumerate(operands)]
    held = [x for x in scratch if getattr(x, "dtype", None) in (BF16, F32)]
    limit = spare + sum(math.prod(x.shape) * jnp.dtype(x.dtype).itemsize for x in held)
    moved = sum(x.size * x.dtype.itemsize for x in operands)
    return pl.pallas_call(
        body,
        in_specs=[pl.BlockSpec(memory_space=pltpu.HBM if i in apart else pltpu.VMEM) for i in range(len(operands))],
        out_specs=whole(1)[0] if single else whole(len(shapes)),
        out_shape=out_shape,
        scratch_shapes=list(scratch),
        compiler_params=pltpu.CompilerParams(vmem_limit_bytes=limit),
        cost_estimate=pl.CostEstimate(flops=flops, bytes_accessed=moved, transcendentals=0),
        name=name,
    )(*operands)


def pack_body(a_ref, o_ref):
    m, width = a_ref.shape
    rest = m - TILE
    piece = rest * width // TILE
    a = a_ref[...].astype(F32)
    o_ref[:, :width] = a[:TILE].astype(BF16)
    left = [a[TILE:, k * piece : (k + 1) * piece] for k in range(TILE // rest)]
    o_ref[:, width:] = jnp.concatenate(left, axis=0).astype(BF16)


def unpack_rows(block, rest, store):
    width = block.shape[1] * TILE // (TILE + rest)
    piece = rest * width // TILE
    store(0, 0, block[:, :width])
    for k in range(TILE // rest):
        store(TILE, k * piece, block[k * rest : (k + 1) * rest, width:])


def pack_all(total, first, rest, blocks):
    width = total.shape[1]
    piece = rest * width // TILE
    base = blocks * TILE + first * rest
    left = [total[base : base + rest, k * piece : (k + 1) * piece] for k in range(TILE // rest)]
    return total[first * TILE : (first + 1) * TILE, :], jnp.concatenate(left, axis=0)


def dequant_short(codes, scales):
    depth, width = codes.shape
    groups = scales.shape[0]
    spread = jnp.broadcast_to(scales[:, None, :], (groups, depth // groups, width)).astype(BF16)
    return (codes.reshape(groups, depth // groups, width) * spread).reshape(depth, width)


def dequant(codes, scales):
    depth, width = codes.shape
    groups = scales.shape[0]
    shaped = codes.astype(F32).reshape(groups, depth // groups, width)
    return (shaped * scales[:, None, :]).astype(BF16).reshape(depth, width)


def pieces(width, shares):
    tiles, total = width // 128, sum(shares)
    if width % 128 or tiles < total:
        return [(0, width)]
    ends = [tiles * sum(shares[:k]) // total for k in range(len(shares) + 1)]
    return [(128 * a, 128 * (b - a)) for a, b in zip(ends, ends[1:])]


def project(a_ref, codes_ref, at, scales_ref, start, size, product=dequant):
    depth = codes_ref.shape[0]
    block = depth // scales_ref.shape[0]
    rows = divisor(depth, 512, 8 * block)
    total = jnp.zeros((a_ref.shape[0], size), F32)
    for k in range(0, depth, rows):
        w = product(codes_ref[k : k + rows, at : at + size], scales_ref[k // block : (k + rows) // block, start : start + size])
        total += jnp.dot(a_ref[:, k : k + rows], w, preferred_element_type=F32)
    return total


class Copies:
    def __init__(self, *wanted):
        self.waiting, self.started = list(wanted), {}
        self.start()

    def start(self):
        if self.waiting:
            source, start, size, target, at, done = self.waiting.pop(0)
            copy = pltpu.make_async_copy(source.at[:, start : start + size], target.at[:, at : at + size], done)
            copy.start()
            self.started[len(self.started)] = copy

    def wait(self, number):
        while number not in self.started:
            self.start()
        self.started[number].wait()


def gate_body(count, rest, *refs):
    blocks = refs[:count]
    codes, scales, later, acts, own, sent, head, wide, done = refs[count:]
    copy = Copies((later, 0, head.shape[1], head, 0, done))
    total = sum(b.shape[0] for b in blocks) // TILE
    at = 0
    for ref in blocks:
        for i in range(ref.shape[0] // TILE):
            def store(row, column, values):
                first = at * TILE if row == 0 else total * TILE + at * rest
                wide[first : first + values.shape[0], column : column + values.shape[1]] = values
            unpack_rows(ref[i * TILE : (i + 1) * TILE, :].astype(F32), rest, store)
            at += 1
    acts[...] = wide[...].astype(BF16)
    for start, size in pieces(codes.shape[1], (1, 1)):
        total = project(acts, codes, start, scales, start, size, dequant_short)
        own[:, start : start + size] = total
        sent[:, start : start + size] = total.astype(BF16)
    copy.wait(0)


def up_body(cuts, acts, first, codes, scales, later, own, sent, head, done, *tail):
    ahead = first.shape[1]
    ours = [(start, size) for start, size in cuts if start >= ahead]
    wanted = [(codes, start, size, tail[0], start - ahead, done.at[i]) for i, (start, size) in enumerate(ours)]
    copies = Copies(*wanted, (later, 0, head.shape[1], head, 0, done.at[len(ours)]))
    for start, size in cuts:
        if start < ahead:
            total = project(acts, first, start, scales, start, size)
        else:
            copies.wait(ours.index((start, size)))
            total = project(acts, tail[0], start - ahead, scales, start, size)
        copies.start()
        own[:, start : start + size] = total
        sent[:, start : start + size] = total.astype(BF16)
    copies.wait(len(ours))


def emit(terms, blocks, rest, outs):
    width = terms.shape[1]
    kept = outs[0].shape[0] // TILE
    for i in range(blocks):
        main, left = pack_all(terms, i, rest, blocks)
        out, at = (outs[0], i) if i < kept else (outs[1], i - kept)
        out[at * TILE : (at + 1) * TILE, :width] = main.astype(out.dtype)
        out[at * TILE : (at + 1) * TILE, width:] = left.astype(out.dtype)


def first_body(rest, blocks, gate, gate_other, up, up_other, codes, later, scales, *refs):
    *outs, hidden, head, terms, tail, done = refs
    size = codes.shape[1]
    part = size // 2
    copies = Copies(
        (later, size, part, tail, 0, done.at[0]),
        (later, size + part, part, tail, part, done.at[1]),
        (later, 2 * size, size, head, 0, done.at[2]),
    )
    width = divisor(hidden.shape[1], 512, 128)
    for c in range(0, hidden.shape[1], width):
        cols = slice(c, c + width)
        g = gate[:, cols] + gate_other[:, cols].astype(F32)
        u = up[:, cols] + up_other[:, cols].astype(F32)
        hidden[:, cols] = (jax.nn.silu(g) * u).astype(BF16)
    copies.start()
    for k in range(2):
        terms[:, k * part : (k + 1) * part] = project(hidden, codes, k * part, scales, k * part, part)
        copies.start()
    for k in range(2):
        copies.wait(k)
        terms[:, size + k * part : size + (k + 1) * part] = project(hidden, tail, k * part, scales, size + k * part, part)
    emit(terms, blocks, rest, outs)
    copies.wait(2)


def second_body(rest, blocks, hidden, codes, later, scales, *refs):
    *outs, terms, tail, done = refs
    size = codes.shape[1]
    part = size // 2
    copies = Copies(*[(later, 3 * size + k * part, part, tail, k * part, done.at[k]) for k in range(2)])
    for k in range(2):
        terms[:, k * part : (k + 1) * part] = project(hidden, codes, k * part, scales, 2 * size + k * part, part)
        copies.start()
    for k in range(2):
        copies.wait(k)
        terms[:, size + k * part : size + (k + 1) * part] = project(hidden, tail, k * part, scales, 3 * size + k * part, part)
    emit(terms, blocks, rest, outs)


def add_body(count, *refs):
    halves, outs = refs[: 2 * count], refs[2 * count :]
    width = halves[0].shape[1]
    for i, ref in enumerate(outs):
        rows = slice(i * TILE, (i + 1) * TILE)
        for k in range(count):
            total = halves[2 * k][rows, :] + halves[2 * k + 1][rows, :].astype(F32)
            ref[:, k * width : (k + 1) * width] = total.astype(ref.dtype)


def last_body(halves, *refs):
    out, count = refs[-1], len(refs) // halves
    width = out.shape[1] // halves
    for k in range(halves):
        terms = refs[k * count : (k + 1) * count]
        total = terms[0][...]
        for ref in terms[1:]:
            total += ref[...].astype(F32)

        def store(row, column, values):
            column += k * width
            out[row : row + values.shape[0], column : column + values.shape[1]] = values.astype(out.dtype)

        unpack_rows(total, out.shape[0] - TILE, store)


def local(peers, acts, gate_codes, gate_scales, up_codes, up_scales, down_codes, down_scales):
    m, width = acts.shape
    units = gate_codes.shape[1]
    rest = m - TILE
    dense = width + rest * width // TILE
    rows = peers * m
    sds = jax.ShapeDtypeStruct
    pair = peers == 8
    far = peers // 2

    def flip(x):
        return lax.ppermute(x, "hidden", [(h, h ^ 1) for h in range(peers)])

    def along(x, s):
        return lax.ppermute(x, "hidden", [(h, (h + 2 * s) % peers) for h in range(peers)])

    def swap(x):
        return lax.ppermute(x, "width", [(0, 1), (1, 0)])

    def in_vmem(x):
        return pltpu.with_memory_space_constraint(x, pltpu.VMEM)

    packed = call(pack_body, sds((TILE, dense), BF16), [acts], "pack", flops=PACK_WEIGHT)
    if pair:
        line = [packed] + [along(packed, s) for s in range(1, far)]
        across = flip(packed)
        blocks = line + [across] + [along(across, s) if s == 2 else flip(line[s]) for s in range(1, far)]
    else:
        blocks = [lax.all_gather(packed, "hidden", axis=0, tiled=True)]
    spare = 2 * MIB + 4096 * rows
    half, packed_half = width // 2, dense // 2
    quarter = half // 2
    cuts = pieces(units, (1, 1, 1, 1))
    ahead = sum(size for _, size in cuts[:2])
    acts_all, gate, gate_sent, up_head = call(
        functools.partial(gate_body, len(blocks), rest),
        [sds((rows, width), BF16), sds((rows, units), F32), sds((rows, units), BF16), pltpu.VMEM((width, ahead), BF16)],
        blocks + [in_vmem(gate_codes), gate_scales, up_codes],
        "gate",
        scratch=[pltpu.VMEM((rows, width), F32), pltpu.SemaphoreType.DMA],
        flops=GATE_WEIGHT,
        spare=spare,
        apart=(len(blocks) + 2,),
    )
    gate_other = swap(gate_sent)
    tail = [pltpu.VMEM((width, units - ahead), BF16)] if ahead < units else []
    up, up_sent, down_head = call(
        functools.partial(up_body, cuts),
        [sds((rows, units), F32), sds((rows, units), BF16), pltpu.VMEM((units, quarter), BF16)],
        [acts_all, in_vmem(up_head), up_codes, up_scales, down_codes],
        "up",
        scratch=[pltpu.SemaphoreType.DMA((max(len(cuts) - 1, 1),))] + tail,
        flops=UP_WEIGHT,
        spare=spare + 4 * MIB,
        apart=(2, 4),
    )
    up_other = swap(up_sent)
    kept = far if pair else peers
    outs = [sds((kept * TILE, packed_half), F32)] + ([sds((far * TILE, packed_half), BF16)] if pair else [])
    work = rows * width * units
    *first, hidden, down_rest = call(
        functools.partial(first_body, rest, peers),
        outs + [sds((rows, units), BF16), pltpu.VMEM((units, quarter), BF16)],
        [gate, gate_other, up, up_other, in_vmem(down_head), down_codes, down_scales],
        "first",
        scratch=[pltpu.VMEM((rows, half), F32), pltpu.VMEM((units, quarter), BF16), pltpu.SemaphoreType.DMA((3,))],
        flops=work,
        spare=spare,
        apart=(5,),
    )
    if pair:
        first_other = flip(first[1])
    second = call(
        functools.partial(second_body, rest, peers),
        outs,
        [hidden, in_vmem(down_rest), down_codes, down_scales],
        "second",
        scratch=[pltpu.VMEM((rows, half), F32), pltpu.VMEM((units, quarter), BF16), pltpu.SemaphoreType.DMA((2,))],
        flops=work,
        spare=spare,
        apart=(2,),
    )
    if pair:
        terms = []
        for mine, other in ((first[0], first_other), (second[0], flip(second[1]))):
            sums = call(
                functools.partial(add_body, 1),
                [sds((TILE, packed_half), F32)] + [sds((TILE, packed_half), BF16)] * (far - 1),
                [mine, other],
                "add",
            )
            terms += [sums[0]] + [along(x, far - s) for s, x in zip(range(1, far), sums[1:])]
    else:
        both = [lax.psum_scatter(x[0], "hidden", scatter_dimension=0, tiled=True) for x in (first, second)]
        terms = both
    return call(functools.partial(last_body, 2), sds((m, width), BF16), terms, "last")


def solution(mesh):
    placed = (
        P(("replica", "hidden"), "width"),
        P("width", "hidden"),
        P("width", "hidden"),
        P("width", "hidden"),
        P("width", "hidden"),
        P("hidden", "width"),
        P("hidden", "width"),
    )
    return jax.shard_map(
        functools.partial(local, mesh.shape["hidden"]),
        mesh=mesh,
        in_specs=placed,
        out_specs=P(("replica", "hidden"), "width"),
        check_vma=False,
    )
```

```python
import functools
import math

import jax
import jax.numpy as jnp
from jax import lax
from jax.experimental import pallas as pl
from jax.experimental.pallas import tpu as pltpu
from jax.sharding import PartitionSpec as P

BF16, F32 = jnp.bfloat16, jnp.float32
MIB = 1 << 20
PACK_WEIGHT, GATE_WEIGHT, UP_WEIGHT = 60_000_000_000, 10_000_000_000, 10_000_000_000
TILE = 8


def divisor(extent, limit, step):
    for size in range(limit - limit % step, 0, -step):
        if extent % size == 0:
            return size
    return extent


def whole(count):
    return [pl.BlockSpec(memory_space=pltpu.VMEM)] * count


def call(body, out_shape, operands, name, scratch=(), flops=0, apart=(), spare=2 * MIB):
    single = not isinstance(out_shape, list)
    shapes = [out_shape] if single else out_shape
    operands = [pltpu.with_memory_space_constraint(x, pltpu.HBM) if i in apart else x for i, x in enumerate(operands)]
    held = [x for x in scratch if getattr(x, "dtype", None) in (BF16, F32)]
    limit = spare + sum(math.prod(x.shape) * jnp.dtype(x.dtype).itemsize for x in held)
    moved = sum(x.size * x.dtype.itemsize for x in operands)
    return pl.pallas_call(
        body,
        in_specs=[pl.BlockSpec(memory_space=pltpu.HBM if i in apart else pltpu.VMEM) for i in range(len(operands))],
        out_specs=whole(1)[0] if single else whole(len(shapes)),
        out_shape=out_shape,
        scratch_shapes=list(scratch),
        compiler_params=pltpu.CompilerParams(vmem_limit_bytes=limit),
        cost_estimate=pl.CostEstimate(flops=flops, bytes_accessed=moved, transcendentals=0),
        name=name,
    )(*operands)


def pack_body(a_ref, o_ref):
    m, width = a_ref.shape
    rest = m - TILE
    piece = rest * width // TILE
    a = a_ref[...].astype(F32)
    o_ref[:, :width] = a[:TILE].astype(BF16)
    left = [a[TILE:, k * piece : (k + 1) * piece] for k in range(TILE // rest)]
    o_ref[:, width:] = jnp.concatenate(left, axis=0).astype(BF16)


def unpack_rows(block, rest, store):
    width = block.shape[1] * TILE // (TILE + rest)
    piece = rest * width // TILE
    store(0, 0, block[:, :width])
    for k in range(TILE // rest):
        store(TILE, k * piece, block[k * rest : (k + 1) * rest, width:])


def pack_all(total, first, rest, blocks):
    width = total.shape[1]
    piece = rest * width // TILE
    base = blocks * TILE + first * rest
    left = [total[base : base + rest, k * piece : (k + 1) * piece] for k in range(TILE // rest)]
    return total[first * TILE : (first + 1) * TILE, :], jnp.concatenate(left, axis=0)


def dequant_short(codes, scales):
    depth, width = codes.shape
    groups = scales.shape[0]
    spread = jnp.broadcast_to(scales[:, None, :], (groups, depth // groups, width)).astype(BF16)
    return (codes.reshape(groups, depth // groups, width) * spread).reshape(depth, width)


def dequant(codes, scales):
    depth, width = codes.shape
    groups = scales.shape[0]
    shaped = codes.astype(F32).reshape(groups, depth // groups, width)
    return (shaped * scales[:, None, :]).astype(BF16).reshape(depth, width)


def pieces(width, shares):
    tiles, total = width // 128, sum(shares)
    if width % 128 or tiles < total:
        return [(0, width)]
    ends = [tiles * sum(shares[:k]) // total for k in range(len(shares) + 1)]
    return [(128 * a, 128 * (b - a)) for a, b in zip(ends, ends[1:])]


def project(a_ref, codes_ref, at, scales_ref, start, size, product=dequant):
    depth = codes_ref.shape[0]
    block = depth // scales_ref.shape[0]
    rows = divisor(depth, 512, 8 * block)
    total = jnp.zeros((a_ref.shape[0], size), F32)
    for k in range(0, depth, rows):
        w = product(codes_ref[k : k + rows, at : at + size], scales_ref[k // block : (k + rows) // block, start : start + size])
        total += jnp.dot(a_ref[:, k : k + rows], w, preferred_element_type=F32)
    return total


class Copies:
    def __init__(self, *wanted):
        self.waiting, self.started = list(wanted), {}
        self.start()

    def start(self):
        if self.waiting:
            source, start, size, target, at, done = self.waiting.pop(0)
            copy = pltpu.make_async_copy(source.at[:, start : start + size], target.at[:, at : at + size], done)
            copy.start()
            self.started[len(self.started)] = copy

    def wait(self, number):
        while number not in self.started:
            self.start()
        self.started[number].wait()


def gate_body(count, rest, *refs):
    blocks = refs[:count]
    codes, scales, later, acts, own, sent, head, wide, done = refs[count:]
    copy = Copies((later, 0, head.shape[1], head, 0, done))
    total = sum(b.shape[0] for b in blocks) // TILE
    at = 0
    for ref in blocks:
        for i in range(ref.shape[0] // TILE):
            def store(row, column, values):
                first = at * TILE if row == 0 else total * TILE + at * rest
                wide[first : first + values.shape[0], column : column + values.shape[1]] = values
            unpack_rows(ref[i * TILE : (i + 1) * TILE, :].astype(F32), rest, store)
            at += 1
    acts[...] = wide[...].astype(BF16)
    for start, size in pieces(codes.shape[1], (1, 1)):
        total = project(acts, codes, start, scales, start, size, dequant_short)
        own[:, start : start + size] = total
        sent[:, start : start + size] = total.astype(BF16)
    copy.wait(0)


def up_body(cuts, acts, first, codes, scales, later, own, sent, head, done, *tail):
    ahead = first.shape[1]
    ours = [(start, size) for start, size in cuts if start >= ahead]
    wanted = [(codes, start, size, tail[0], start - ahead, done.at[i]) for i, (start, size) in enumerate(ours)]
    copies = Copies(*wanted, (later, 0, head.shape[1], head, 0, done.at[len(ours)]))
    for start, size in cuts:
        if start < ahead:
            total = project(acts, first, start, scales, start, size)
        else:
            copies.wait(ours.index((start, size)))
            total = project(acts, tail[0], start - ahead, scales, start, size)
        copies.start()
        own[:, start : start + size] = total
        sent[:, start : start + size] = total.astype(BF16)
    copies.wait(len(ours))


def emit(terms, blocks, rest, outs):
    width = terms.shape[1]
    kept = outs[0].shape[0] // TILE
    for i in range(blocks):
        main, left = pack_all(terms, i, rest, blocks)
        out, at = (outs[0], i) if i < kept else (outs[1], i - kept)
        out[at * TILE : (at + 1) * TILE, :width] = main.astype(out.dtype)
        out[at * TILE : (at + 1) * TILE, width:] = left.astype(out.dtype)


def first_body(rest, blocks, gate, gate_other, up, up_other, codes, later, scales, *refs):
    *outs, hidden, head, terms, tail, done = refs
    size = codes.shape[1]
    part = size // 2
    copies = Copies(
        (later, size, part, tail, 0, done.at[0]),
        (later, size + part, part, tail, part, done.at[1]),
        (later, 2 * size, size, head, 0, done.at[2]),
    )
    width = divisor(hidden.shape[1], 512, 128)
    for c in range(0, hidden.shape[1], width):
        cols = slice(c, c + width)
        g = gate[:, cols] + gate_other[:, cols].astype(F32)
        u = up[:, cols] + up_other[:, cols].astype(F32)
        hidden[:, cols] = (jax.nn.silu(g) * u).astype(BF16)
    copies.start()
    for k in range(2):
        terms[:, k * part : (k + 1) * part] = project(hidden, codes, k * part, scales, k * part, part, dequant_short)
        copies.start()
    for k in range(2):
        copies.wait(k)
        terms[:, size + k * part : size + (k + 1) * part] = project(hidden, tail, k * part, scales, size + k * part, part, dequant_short)
    emit(terms, blocks, rest, outs)
    copies.wait(2)


def second_body(rest, blocks, hidden, codes, later, scales, *refs):
    *outs, terms, tail, done = refs
    size = codes.shape[1]
    part = size // 2
    copies = Copies(*[(later, 3 * size + k * part, part, tail, k * part, done.at[k]) for k in range(2)])
    for k in range(2):
        terms[:, k * part : (k + 1) * part] = project(hidden, codes, k * part, scales, 2 * size + k * part, part, dequant_short)
        copies.start()
    for k in range(2):
        copies.wait(k)
        terms[:, size + k * part : size + (k + 1) * part] = project(hidden, tail, k * part, scales, 3 * size + k * part, part, dequant_short)
    emit(terms, blocks, rest, outs)


def add_body(count, *refs):
    halves, outs = refs[: 2 * count], refs[2 * count :]
    width = halves[0].shape[1]
    for i, ref in enumerate(outs):
        rows = slice(i * TILE, (i + 1) * TILE)
        for k in range(count):
            total = halves[2 * k][rows, :] + halves[2 * k + 1][rows, :].astype(F32)
            ref[:, k * width : (k + 1) * width] = total.astype(ref.dtype)


def last_body(halves, *refs):
    out, count = refs[-1], len(refs) // halves
    width = out.shape[1] // halves
    for k in range(halves):
        terms = refs[k * count : (k + 1) * count]
        total = terms[0][...]
        for ref in terms[1:]:
            total += ref[...].astype(F32)

        def store(row, column, values):
            column += k * width
            out[row : row + values.shape[0], column : column + values.shape[1]] = values.astype(out.dtype)

        unpack_rows(total, out.shape[0] - TILE, store)


def local(peers, acts, gate_codes, gate_scales, up_codes, up_scales, down_codes, down_scales):
    m, width = acts.shape
    units = gate_codes.shape[1]
    rest = m - TILE
    dense = width + rest * width // TILE
    rows = peers * m
    sds = jax.ShapeDtypeStruct
    pair = peers == 8
    far = peers // 2

    def flip(x):
        return lax.ppermute(x, "hidden", [(h, h ^ 1) for h in range(peers)])

    def along(x, s):
        return lax.ppermute(x, "hidden", [(h, (h + 2 * s) % peers) for h in range(peers)])

    def swap(x):
        return lax.ppermute(x, "width", [(0, 1), (1, 0)])

    def in_vmem(x):
        return pltpu.with_memory_space_constraint(x, pltpu.VMEM)

    packed = call(pack_body, sds((TILE, dense), BF16), [acts], "pack", flops=PACK_WEIGHT)
    if pair:
        line = [packed] + [along(packed, s) for s in range(1, far)]
        across = flip(packed)
        blocks = line + [across] + [along(across, s) if s == 2 else flip(line[s]) for s in range(1, far)]
    else:
        blocks = [lax.all_gather(packed, "hidden", axis=0, tiled=True)]
    spare = 2 * MIB + 4096 * rows
    half, packed_half = width // 2, dense // 2
    quarter = half // 2
    cuts = pieces(units, (1, 1, 1, 1))
    ahead = sum(size for _, size in cuts[:2])
    acts_all, gate, gate_sent, up_head = call(
        functools.partial(gate_body, len(blocks), rest),
        [sds((rows, width), BF16), sds((rows, units), F32), sds((rows, units), BF16), pltpu.VMEM((width, ahead), BF16)],
        blocks + [in_vmem(gate_codes), gate_scales, up_codes],
        "gate",
        scratch=[pltpu.VMEM((rows, width), F32), pltpu.SemaphoreType.DMA],
        flops=GATE_WEIGHT,
        spare=spare,
        apart=(len(blocks) + 2,),
    )
    gate_other = swap(gate_sent)
    tail = [pltpu.VMEM((width, units - ahead), BF16)] if ahead < units else []
    up, up_sent, down_head = call(
        functools.partial(up_body, cuts),
        [sds((rows, units), F32), sds((rows, units), BF16), pltpu.VMEM((units, quarter), BF16)],
        [acts_all, in_vmem(up_head), up_codes, up_scales, down_codes],
        "up",
        scratch=[pltpu.SemaphoreType.DMA((max(len(cuts) - 1, 1),))] + tail,
        flops=UP_WEIGHT,
        spare=spare + 4 * MIB,
        apart=(2, 4),
    )
    up_other = swap(up_sent)
    kept = far if pair else peers
    outs = [sds((kept * TILE, packed_half), F32)] + ([sds((far * TILE, packed_half), BF16)] if pair else [])
    work = rows * width * units
    *first, hidden, down_rest = call(
        functools.partial(first_body, rest, peers),
        outs + [sds((rows, units), BF16), pltpu.VMEM((units, quarter), BF16)],
        [gate, gate_other, up, up_other, in_vmem(down_head), down_codes, down_scales],
        "first",
        scratch=[pltpu.VMEM((rows, half), F32), pltpu.VMEM((units, quarter), BF16), pltpu.SemaphoreType.DMA((3,))],
        flops=work,
        spare=spare,
        apart=(5,),
    )
    if pair:
        first_other = flip(first[1])
    second = call(
        functools.partial(second_body, rest, peers),
        outs,
        [hidden, in_vmem(down_rest), down_codes, down_scales],
        "second",
        scratch=[pltpu.VMEM((rows, half), F32), pltpu.VMEM((units, quarter), BF16), pltpu.SemaphoreType.DMA((2,))],
        flops=work,
        spare=spare,
        apart=(2,),
    )
    if pair:
        terms = []
        for mine, other in ((first[0], first_other), (second[0], flip(second[1]))):
            sums = call(
                functools.partial(add_body, 1),
                [sds((TILE, packed_half), F32)] + [sds((TILE, packed_half), BF16)] * (far - 1),
                [mine, other],
                "add",
            )
            terms += [sums[0]] + [along(x, far - s) for s, x in zip(range(1, far), sums[1:])]
    else:
        both = [lax.psum_scatter(x[0], "hidden", scatter_dimension=0, tiled=True) for x in (first, second)]
        terms = both
    return call(functools.partial(last_body, 2), sds((m, width), BF16), terms, "last")


def solution(mesh):
    placed = (
        P(("replica", "hidden"), "width"),
        P("width", "hidden"),
        P("width", "hidden"),
        P("width", "hidden"),
        P("width", "hidden"),
        P("hidden", "width"),
        P("hidden", "width"),
    )
    return jax.shard_map(
        functools.partial(local, mesh.shape["hidden"]),
        mesh=mesh,
        in_specs=placed,
        out_specs=P(("replica", "hidden"), "width"),
        check_vma=False,
    )
```

```python
import functools
import math

import jax
import jax.numpy as jnp
from jax import lax
from jax.experimental import pallas as pl
from jax.experimental.pallas import tpu as pltpu
from jax.sharding import PartitionSpec as P

BF16, F32 = jnp.bfloat16, jnp.float32
MIB = 1 << 20
PACK_WEIGHT, GATE_WEIGHT, UP_WEIGHT = 60_000_000_000, 10_000_000_000, 10_000_000_000
TILE = 8


def divisor(extent, limit, step):
    for size in range(limit - limit % step, 0, -step):
        if extent % size == 0:
            return size
    return extent


def whole(count):
    return [pl.BlockSpec(memory_space=pltpu.VMEM)] * count


def call(body, out_shape, operands, name, scratch=(), flops=0, apart=(), spare=2 * MIB):
    single = not isinstance(out_shape, list)
    shapes = [out_shape] if single else out_shape
    operands = [pltpu.with_memory_space_constraint(x, pltpu.HBM) if i in apart else x for i, x in enumerate(operands)]
    held = [x for x in scratch if getattr(x, "dtype", None) in (BF16, F32)]
    limit = spare + sum(math.prod(x.shape) * jnp.dtype(x.dtype).itemsize for x in held)
    moved = sum(x.size * x.dtype.itemsize for x in operands)
    return pl.pallas_call(
        body,
        in_specs=[pl.BlockSpec(memory_space=pltpu.HBM if i in apart else pltpu.VMEM) for i in range(len(operands))],
        out_specs=whole(1)[0] if single else whole(len(shapes)),
        out_shape=out_shape,
        scratch_shapes=list(scratch),
        compiler_params=pltpu.CompilerParams(vmem_limit_bytes=limit),
        cost_estimate=pl.CostEstimate(flops=flops, bytes_accessed=moved, transcendentals=0),
        name=name,
    )(*operands)


def pack_body(a_ref, o_ref):
    m, width = a_ref.shape
    rest = m - TILE
    piece = rest * width // TILE
    a = a_ref[...].astype(F32)
    o_ref[:, :width] = a[:TILE].astype(BF16)
    left = [a[TILE:, k * piece : (k + 1) * piece] for k in range(TILE // rest)]
    o_ref[:, width:] = jnp.concatenate(left, axis=0).astype(BF16)


def unpack_rows(block, rest, store):
    width = block.shape[1] * TILE // (TILE + rest)
    piece = rest * width // TILE
    store(0, 0, block[:, :width])
    for k in range(TILE // rest):
        store(TILE, k * piece, block[k * rest : (k + 1) * rest, width:])


def pack_all(total, first, rest, blocks):
    width = total.shape[1]
    piece = rest * width // TILE
    base = blocks * TILE + first * rest
    left = [total[base : base + rest, k * piece : (k + 1) * piece] for k in range(TILE // rest)]
    return total[first * TILE : (first + 1) * TILE, :], jnp.concatenate(left, axis=0)


def dequant_short(codes, scales):
    depth, width = codes.shape
    groups = scales.shape[0]
    spread = jnp.broadcast_to(scales[:, None, :], (groups, depth // groups, width)).astype(BF16)
    return (codes.reshape(groups, depth // groups, width) * spread).reshape(depth, width)


def dequant(codes, scales):
    depth, width = codes.shape
    groups = scales.shape[0]
    shaped = codes.astype(F32).reshape(groups, depth // groups, width)
    return (shaped * scales[:, None, :]).astype(BF16).reshape(depth, width)


def pieces(width, shares):
    tiles, total = width // 128, sum(shares)
    if width % 128 or tiles < total:
        return [(0, width)]
    ends = [tiles * sum(shares[:k]) // total for k in range(len(shares) + 1)]
    return [(128 * a, 128 * (b - a)) for a, b in zip(ends, ends[1:])]


def project(a_ref, codes_ref, at, scales_ref, start, size, product=dequant):
    depth = codes_ref.shape[0]
    block = depth // scales_ref.shape[0]
    rows = divisor(depth, 512, 8 * block)
    total = jnp.zeros((a_ref.shape[0], size), F32)
    for k in range(0, depth, rows):
        w = product(codes_ref[k : k + rows, at : at + size], scales_ref[k // block : (k + rows) // block, start : start + size])
        total += jnp.dot(a_ref[:, k : k + rows], w, preferred_element_type=F32)
    return total


class Copies:
    def __init__(self, *wanted):
        self.waiting, self.started = list(wanted), {}
        self.start()

    def start(self):
        if self.waiting:
            source, start, size, target, at, done = self.waiting.pop(0)
            copy = pltpu.make_async_copy(source.at[:, start : start + size], target.at[:, at : at + size], done)
            copy.start()
            self.started[len(self.started)] = copy

    def wait(self, number):
        while number not in self.started:
            self.start()
        self.started[number].wait()


def gate_body(count, rest, *refs):
    blocks = refs[:count]
    codes, scales, later, acts, own, sent, head, wide, done = refs[count:]
    copy = Copies((later, 0, head.shape[1], head, 0, done))
    total = sum(b.shape[0] for b in blocks) // TILE
    at = 0
    for ref in blocks:
        for i in range(ref.shape[0] // TILE):
            def store(row, column, values):
                first = at * TILE if row == 0 else total * TILE + at * rest
                wide[first : first + values.shape[0], column : column + values.shape[1]] = values
            unpack_rows(ref[i * TILE : (i + 1) * TILE, :].astype(F32), rest, store)
            at += 1
    acts[...] = wide[...].astype(BF16)
    for start, size in pieces(codes.shape[1], (1, 1)):
        total = project(acts, codes, start, scales, start, size, dequant_short)
        own[:, start : start + size] = total
        sent[:, start : start + size] = total.astype(BF16)
    copy.wait(0)


def up_body(cuts, acts, first, codes, scales, later, own, sent, head, done, *tail):
    ahead = first.shape[1]
    ours = [(start, size) for start, size in cuts if start >= ahead]
    wanted = [(codes, start, size, tail[0], start - ahead, done.at[i]) for i, (start, size) in enumerate(ours)]
    copies = Copies(*wanted, (later, 0, head.shape[1], head, 0, done.at[len(ours)]))
    for start, size in cuts:
        if start < ahead:
            total = project(acts, first, start, scales, start, size)
        else:
            copies.wait(ours.index((start, size)))
            total = project(acts, tail[0], start - ahead, scales, start, size)
        copies.start()
        own[:, start : start + size] = total
        sent[:, start : start + size] = total.astype(BF16)
    copies.wait(len(ours))


def emit(terms, blocks, rest, outs):
    width = terms.shape[1]
    kept = outs[0].shape[0] // TILE
    for i in range(blocks):
        main, left = pack_all(terms, i, rest, blocks)
        out, at = (outs[0], i) if i < kept else (outs[1], i - kept)
        out[at * TILE : (at + 1) * TILE, :width] = main.astype(out.dtype)
        out[at * TILE : (at + 1) * TILE, width:] = left.astype(out.dtype)


def first_body(rest, blocks, gate, gate_other, up, up_other, codes, later, scales, *refs):
    *outs, hidden, head, terms, tail, done = refs
    size = codes.shape[1]
    part = size // 2
    copies = Copies(
        (later, size, part, tail, 0, done.at[0]),
        (later, size + part, part, tail, part, done.at[1]),
        (later, 2 * size, size, head, 0, done.at[2]),
    )
    width = divisor(hidden.shape[1], 512, 128)
    for c in range(0, hidden.shape[1], width):
        cols = slice(c, c + width)
        g = gate[:, cols] + gate_other[:, cols].astype(F32)
        u = up[:, cols] + up_other[:, cols].astype(F32)
        hidden[:, cols] = (jax.nn.silu(g) * u).astype(BF16)
    copies.start()
    for k in range(2):
        terms[:, k * part : (k + 1) * part] = project(hidden, codes, k * part, scales, k * part, part, dequant_short)
        copies.start()
    for k in range(2):
        copies.wait(k)
        terms[:, size + k * part : size + (k + 1) * part] = project(hidden, tail, k * part, scales, size + k * part, part, dequant_short)
    emit(terms, blocks, rest, outs)
    copies.wait(2)


def second_body(rest, blocks, hidden, codes, later, scales, *refs):
    *outs, terms, tail, done = refs
    size = codes.shape[1]
    part = size // 2
    copies = Copies(*[(later, 3 * size + k * part, part, tail, k * part, done.at[k]) for k in range(2)])
    copies.start()
    for k in range(2):
        terms[:, k * part : (k + 1) * part] = project(hidden, codes, k * part, scales, 2 * size + k * part, part, dequant_short)
        copies.start()
    for k in range(2):
        copies.wait(k)
        terms[:, size + k * part : size + (k + 1) * part] = project(hidden, tail, k * part, scales, 3 * size + k * part, part, dequant_short)
    emit(terms, blocks, rest, outs)


def add_body(count, *refs):
    halves, outs = refs[: 2 * count], refs[2 * count :]
    width = halves[0].shape[1]
    for i, ref in enumerate(outs):
        rows = slice(i * TILE, (i + 1) * TILE)
        for k in range(count):
            total = halves[2 * k][rows, :] + halves[2 * k + 1][rows, :].astype(F32)
            ref[:, k * width : (k + 1) * width] = total.astype(ref.dtype)


def last_body(halves, *refs):
    out, count = refs[-1], len(refs) // halves
    width = out.shape[1] // halves
    for k in range(halves):
        terms = refs[k * count : (k + 1) * count]
        total = terms[0][...]
        for ref in terms[1:]:
            total += ref[...].astype(F32)

        def store(row, column, values):
            column += k * width
            out[row : row + values.shape[0], column : column + values.shape[1]] = values.astype(out.dtype)

        unpack_rows(total, out.shape[0] - TILE, store)


def local(peers, acts, gate_codes, gate_scales, up_codes, up_scales, down_codes, down_scales):
    m, width = acts.shape
    units = gate_codes.shape[1]
    rest = m - TILE
    dense = width + rest * width // TILE
    rows = peers * m
    sds = jax.ShapeDtypeStruct
    pair = peers == 8
    far = peers // 2

    def flip(x):
        return lax.ppermute(x, "hidden", [(h, h ^ 1) for h in range(peers)])

    def along(x, s):
        return lax.ppermute(x, "hidden", [(h, (h + 2 * s) % peers) for h in range(peers)])

    def swap(x):
        return lax.ppermute(x, "width", [(0, 1), (1, 0)])

    def in_vmem(x):
        return pltpu.with_memory_space_constraint(x, pltpu.VMEM)

    packed = call(pack_body, sds((TILE, dense), BF16), [acts], "pack", flops=PACK_WEIGHT)
    if pair:
        line = [packed] + [along(packed, s) for s in range(1, far)]
        across = flip(packed)
        blocks = line + [across] + [along(across, s) if s == 2 else flip(line[s]) for s in range(1, far)]
    else:
        blocks = [lax.all_gather(packed, "hidden", axis=0, tiled=True)]
    spare = 2 * MIB + 4096 * rows
    half, packed_half = width // 2, dense // 2
    quarter = half // 2
    cuts = pieces(units, (1, 1, 1, 1))
    ahead = sum(size for _, size in cuts[:2])
    acts_all, gate, gate_sent, up_head = call(
        functools.partial(gate_body, len(blocks), rest),
        [sds((rows, width), BF16), sds((rows, units), F32), sds((rows, units), BF16), pltpu.VMEM((width, ahead), BF16)],
        blocks + [in_vmem(gate_codes), gate_scales, up_codes],
        "gate",
        scratch=[pltpu.VMEM((rows, width), F32), pltpu.SemaphoreType.DMA],
        flops=GATE_WEIGHT,
        spare=spare,
        apart=(len(blocks) + 2,),
    )
    gate_other = swap(gate_sent)
    tail = [pltpu.VMEM((width, units - ahead), BF16)] if ahead < units else []
    up, up_sent, down_head = call(
        functools.partial(up_body, cuts),
        [sds((rows, units), F32), sds((rows, units), BF16), pltpu.VMEM((units, quarter), BF16)],
        [acts_all, in_vmem(up_head), up_codes, up_scales, down_codes],
        "up",
        scratch=[pltpu.SemaphoreType.DMA((max(len(cuts) - 1, 1),))] + tail,
        flops=UP_WEIGHT,
        spare=spare + 4 * MIB,
        apart=(2, 4),
    )
    up_other = swap(up_sent)
    kept = far if pair else peers
    outs = [sds((kept * TILE, packed_half), F32)] + ([sds((far * TILE, packed_half), BF16)] if pair else [])
    work = rows * width * units
    *first, hidden, down_rest = call(
        functools.partial(first_body, rest, peers),
        outs + [sds((rows, units), BF16), pltpu.VMEM((units, quarter), BF16)],
        [gate, gate_other, up, up_other, in_vmem(down_head), down_codes, down_scales],
        "first",
        scratch=[pltpu.VMEM((rows, half), F32), pltpu.VMEM((units, quarter), BF16), pltpu.SemaphoreType.DMA((3,))],
        flops=work,
        spare=spare,
        apart=(5,),
    )
    if pair:
        first_other = flip(first[1])
    second = call(
        functools.partial(second_body, rest, peers),
        outs,
        [hidden, in_vmem(down_rest), down_codes, down_scales],
        "second",
        scratch=[pltpu.VMEM((rows, half), F32), pltpu.VMEM((units, quarter), BF16), pltpu.SemaphoreType.DMA((2,))],
        flops=work,
        spare=spare,
        apart=(2,),
    )
    if pair:
        terms = []
        for mine, other in ((first[0], first_other), (second[0], flip(second[1]))):
            sums = call(
                functools.partial(add_body, 1),
                [sds((TILE, packed_half), F32)] + [sds((TILE, packed_half), BF16)] * (far - 1),
                [mine, other],
                "add",
            )
            terms += [sums[0]] + [along(x, far - s) for s, x in zip(range(1, far), sums[1:])]
    else:
        both = [lax.psum_scatter(x[0], "hidden", scatter_dimension=0, tiled=True) for x in (first, second)]
        terms = both
    return call(functools.partial(last_body, 2), sds((m, width), BF16), terms, "last")


def solution(mesh):
    placed = (
        P(("replica", "hidden"), "width"),
        P("width", "hidden"),
        P("width", "hidden"),
        P("width", "hidden"),
        P("width", "hidden"),
        P("hidden", "width"),
        P("hidden", "width"),
    )
    return jax.shard_map(
        functools.partial(local, mesh.shape["hidden"]),
        mesh=mesh,
        in_specs=placed,
        out_specs=P(("replica", "hidden"), "width"),
        check_vma=False,
    )
```
